256 devices in a mesh: rows: 16 (over z_hi, x), cols: 4 (over z_lo, core), depth: 4 (over y).
Axes of the slice: x: 4, y: 4, z: 8 (z_hi: 4, z_lo: 2; z = z_hi * 2 + z_lo), core: 2. Of those that a mesh axis runs over, the one named last changes fastest.
Arguments:
- tokens_in: bfloat16 [256, 8192], P('rows', 'depth'), may hold values from -6 to 6
- cotangent: bfloat16 [256, 8192], P('rows', 'depth'), may hold values from -1.5 to 1.5
- w_gate: bfloat16 [8192, 28672], P('depth', ('rows', 'cols')), may hold values from -0.0625 to 0.0625
- w_up: bfloat16 [8192, 28672], P('depth', ('rows', 'cols')), may hold values from -0.0625 to 0.0625
- w_down: bfloat16 [28672, 8192], P(('rows', 'cols'), 'depth'), may hold values from -0.03125 to 0.03125
Outputs:
- block_out: bfloat16 [256, 8192], P(('rows', 'cols'), 'depth')
- input_grad: bfloat16 [256, 8192], P(('rows', 'cols'), 'depth')
- gate_grad: bfloat16 [8192, 28672], P('depth', ('rows', 'cols'))
- up_grad: bfloat16 [8192, 28672], P('depth', ('rows', 'cols'))
- down_grad: bfloat16 [28672, 8192], P(('rows', 'cols'), 'depth')
The draws below stay inside these ranges and needn't reach their ends.
All inputs are finite; a program needn't handle non-finite values.
Results may differ from the reference program's by a relative error of at most 0.0049.
Values may be sent and summed in bfloat16 or wider, within the bound.
A program may use at most 64 MiB of HBM per device.

```python
import jax
import jax.numpy as jnp
from jax import lax

D = 8192
F = 28672
TOKENS = 256


def steps_of(stream_key, extent, split, smallest, high):
    def one(dim, shards_of):
        steps = jax.random.uniform(jax.random.fold_in(jax.random.fold_in(stream_key, 6), dim), (shards_of,), jnp.float32, smallest / len(split), high / len(split))
        return jnp.repeat(jnp.exp(steps), extent[dim] // shards_of).reshape((-1,) + (1,) * (len(extent) - dim - 1))

    gain = one(*split[0])
    for cut in split[1:]:
        gain = gain * one(*cut)
    return gain


def scatter_about(own_key, dims, scale, bound, split=(), kind=jnp.bfloat16):
    array = scale * jax.random.normal(own_key, dims, jnp.float32)
    if split:
        array = array * steps_of(own_key, dims, split, -0.22, 0.18)
    return jnp.clip(array, -bound, bound).astype(kind)


def setup_inputs(seed: int = 0) -> dict:
    streams_of = jax.random.split(jax.random.key(seed), 6)
    return {
        "tokens_in": scatter_about(streams_of[0], (TOKENS, D), 1.0, 6.0, ((0, 16), (1, 4))),
        "cotangent": scatter_about(streams_of[1], (TOKENS, D), 0.25, 1.5, ((0, 16), (1, 4))),
        "w_gate": scatter_about(streams_of[2], (D, F), D ** -0.5, 0.0625, ((0, 4), (1, 64))),
        "w_up": scatter_about(streams_of[3], (D, F), D ** -0.5, 0.0625, ((0, 4), (1, 64))),
        "w_down": scatter_about(streams_of[4], (F, D), F ** -0.5, 0.03125, ((0, 64), (1, 4))),
    }


def backward_local(hidden_back, gate, up):
    sigma = jax.nn.sigmoid(gate)
    up_back = (hidden_back * gate * sigma).astype(jnp.bfloat16)
    gate_back = (hidden_back * up * sigma * (1.0 + gate * (1.0 - sigma))).astype(jnp.bfloat16)
    return gate_back, up_back


def reference(tokens_in, cotangent, w_gate, w_up, w_down):
    gate = jnp.dot(tokens_in, w_gate, preferred_element_type=jnp.float32)
    up = jnp.dot(tokens_in, w_up, preferred_element_type=jnp.float32)
    hidden = (jax.nn.silu(gate) * up).astype(jnp.bfloat16)
    block_out = jnp.dot(hidden, w_down, preferred_element_type=jnp.float32).astype(jnp.bfloat16)
    hidden_back = lax.dot_general(cotangent, w_down, (((1,), (1,)), ((), ())), preferred_element_type=jnp.float32)
    gate_back, up_back = backward_local(hidden_back, gate, up)
    input_grad = lax.dot_general(gate_back, w_gate, (((1,), (1,)), ((), ())), preferred_element_type=jnp.float32)
    input_grad = input_grad + lax.dot_general(up_back, w_up, (((1,), (1,)), ((), ())), preferred_element_type=jnp.float32)
    gate_grad = lax.dot_general(tokens_in, gate_back, (((0,), (0,)), ((), ())), preferred_element_type=jnp.float32).astype(jnp.bfloat16)
    up_grad = lax.dot_general(tokens_in, up_back, (((0,), (0,)), ((), ())), preferred_element_type=jnp.float32).astype(jnp.bfloat16)
    down_grad = lax.dot_general(hidden, cotangent, (((0,), (0,)), ((), ())), preferred_element_type=jnp.float32).astype(jnp.bfloat16)
    return block_out, input_grad.astype(jnp.bfloat16), gate_grad, up_grad, down_grad
```

```python
import functools

import jax
import jax.numpy as jnp
from jax import lax
from jax.experimental import pallas as pl
from jax.experimental.pallas import tpu as pltpu
from jax.sharding import PartitionSpec as P

MESH = pl.DeviceIdType.MESH
F32 = jnp.float32
BF16 = jnp.bfloat16
NQ = 4
NX = 4
NY = 4
NC = 2
QC = NQ // NC
ROWS = 16


def contract_last(left, right):
    return lax.dot_general(
        left, right, (((1,), (1,)), ((), ())), preferred_element_type=F32
    )


def contract_first(left, right):
    return lax.dot_general(
        left, right, (((0,), (0,)), ((), ())), preferred_element_type=F32
    )


def block_kernel(
    tokens_ref, cot_ref, w_gate_ref, w_up_ref, w_down_ref,
    out_ref, back_ref, tok_out, act_out,
    tok, wg, wu, wd, part32, part16, part_in, act,
    core_send, core_in, own, xsend, xin, zown, zsend, zin, fin,
    load_sem, zs, zr, xs, xr, cs, cr, ys, yr, hs, hr, os_, or_, us, ur, vs, vr, fs, fr, st_sem,
):
    r, c, y = lax.axis_index("rows"), lax.axis_index("cols"), lax.axis_index("depth")
    z_hi, x = r // NX, r % NX
    z_lo, core = c // 2, c % 2
    half = tok.shape[-1]
    f = wg.shape[-1]
    quarter = half // 2

    def at(dz=0, dx=0, lo=None, k=None, dy=0):
        lo = z_lo if lo is None else lo
        k = core if k is None else k
        row = lax.rem(z_hi + dz, NQ) * NX + lax.rem(x + dx, NX)
        return (row, lo * 2 + k, lax.rem(y + dy, NY))

    loads = []
    for h in range(2):
        place = pl.multiple_of((core + h) % 2 * half, half)
        loads.append([
            pltpu.make_async_copy(w_gate_ref.at[pl.ds(place, half), :], wg.at[h], load_sem.at[h, 0]),
            pltpu.make_async_copy(w_up_ref.at[pl.ds(place, half), :], wu.at[h], load_sem.at[h, 1]),
            pltpu.make_async_copy(w_down_ref.at[:, pl.ds(place, half)], wd.at[h], load_sem.at[h, 2]),
        ])
    for group in loads:
        for load in group:
            load.start()

    barrier = pltpu.get_barrier_semaphore()
    partners = [at(dx=d) for d in range(1, NX)] + [at(dy=d) for d in range(1, NY)]
    partners += [at(dz=d, lo=lo) for d in range(1, NQ) for lo in range(2)]
    partners += [at(lo=1 - z_lo), at(k=1 - core), at(lo=1 - z_lo, k=1 - core)]
    for partner in partners:
        pl.semaphore_signal(barrier, inc=1, device_id=partner, device_id_type=MESH)

    mine = pl.ds(pl.multiple_of(core * half, half), half)
    tok[0, 0, 0, 0:ROWS] = tokens_ref[:, mine]
    tok[0, 1, 0, 0:ROWS] = cot_ref[:, mine]
    pl.semaphore_wait(barrier, len(partners))

    sends = []

    def send(src, dst, ss, rs, to):
        copy = pltpu.make_async_remote_copy(
            src_ref=src, dst_ref=dst, send_sem=ss, recv_sem=rs, device_id=to, device_id_type=MESH
        )
        copy.start()
        sends.append(copy)

    def arrived(dst, ss, rs, to):
        pltpu.make_async_remote_copy(
            src_ref=dst, dst_ref=dst, send_sem=ss, recv_sem=rs, device_id=to, device_id_type=MESH
        ).wait_recv()

    shift = 1 + 2 * (1 - z_lo)
    slot = 4 - shift
    own_shard = tok.at[0, :, 0, pl.ds(0, ROWS)]
    for lo in range(2):
        send(own_shard, tok.at[0, :, slot, pl.ds(0, ROWS)], zs.at[lo], zr.at[slot], at(dz=shift, lo=lo))
    send(own_shard, tok.at[0, :, 2, pl.ds(0, ROWS)], zs.at[2], zr.at[2], at(dz=2, lo=1 - z_lo))

    def stage_x(q):
        if q:
            arrived(tok.at[0, :, q, pl.ds(0, ROWS)], zs.at[0], zr.at[q], at(dx=1))
        for d in range(1, NX):
            p = NX - d
            send(
                tok.at[0, :, q, pl.ds(0, ROWS)], tok.at[0, :, q, pl.ds(p * ROWS, ROWS)],
                xs.at[q, d], xr.at[q, p], at(dx=d),
            )

    def stage_core(q):
        for p in range(1, NX):
            arrived(tok.at[0, :, q, pl.ds(p * ROWS, ROWS)], xs.at[q, p], xr.at[q, p], at(dx=1))
        send(tok.at[0, :, q], tok.at[1, :, q], cs.at[q], cr.at[q], at(k=1 - core))

    rows = QC * NX * ROWS
    share = rows // NY

    def stage_mm(n):
        gs = pl.ds(n * QC, QC)
        sums = []
        for h in range(2):
            if n == 0:
                for load in loads[h]:
                    load.wait()
            if h:
                for q in range(n * QC, n * QC + QC):
                    arrived(tok.at[1, :, q], cs.at[q], cr.at[q], at(k=1 - core))
            t = tok[h, 0, gs].reshape(rows, half)
            g = tok[h, 1, gs].reshape(rows, half)
            terms = [
                jnp.dot(t, wg[h], preferred_element_type=F32),
                jnp.dot(t, wu[h], preferred_element_type=F32),
                contract_last(g, wd[h]),
            ]
            for i, term in enumerate(terms):
                term = term.reshape(NY, share, f)
                if h:
                    term = term + part32[n, :, i]
                    part16[n, :, i] = term.astype(BF16)
                part32[n, :, i] = term
        for d in range(1, NY):
            to = lax.rem(y + d, NY)
            send(part16.at[n, to], part_in.at[n, NY - d - 1], ys.at[n, d], yr.at[n, NY - d], at(dy=d))

    def stage_act(n):
        for p in range(1, NY):
            arrived(part_in.at[n, p - 1], ys.at[n, p], yr.at[n, p], at(dy=1))
        gate, up, hidden_back = [
            part32[n, y, i] + (part_in[n, 0, i].astype(F32) + part_in[n, 1, i].astype(F32)
                               + part_in[n, 2, i].astype(F32))
            for i in range(3)
        ]
        sigma = jax.nn.sigmoid(gate)
        act[n, y, 0] = (gate * sigma * up).astype(BF16)
        act[n, y, 1] = (hidden_back * up * sigma * (1.0 + gate * (1.0 - sigma))).astype(BF16)
        act[n, y, 2] = (hidden_back * gate * sigma).astype(BF16)
        for d in range(1, NY):
            send(act.at[n, y], act.at[n, y], hs.at[n, d], hr.at[n, NY - d], at(dy=d))

    def stage_out(n):
        for p in range(1, NY):
            arrived(act.at[n, lax.rem(y + p, NY)], hs.at[n, p], hr.at[n, p], at(dy=1))
        hidden, gate_back, up_back = [act[n, :, i].reshape(rows, f) for i in range(3)]

        def outputs(h):
            return [
                jnp.dot(hidden, wd[h], preferred_element_type=F32),
                contract_last(gate_back, wg[h]) + contract_last(up_back, wu[h]),
            ]

        for i, value in enumerate(outputs(1)):
            core_send[n, i] = value.astype(core_send.dtype)
        send(core_send.at[n], core_in.at[n], os_.at[n], or_.at[n], at(k=1 - core))
        values = outputs(0)
        arrived(core_in.at[n], os_.at[n], or_.at[n], at(k=1 - core))
        for i, value in enumerate(values):
            value = (value + core_in[n, i].astype(F32)).reshape(QC, NX, ROWS, half)
            own[n, i] = value[:, 0]
            for p in range(1, NX):
                xsend[n, p - 1, i] = value[:, p].astype(BF16)
        for d in range(1, NX):
            send(xsend.at[n, d - 1], xin.at[n, NX - d - 1], us.at[n, d], ur.at[n, NX - d], at(dx=d))

    def stage_z(n):
        for p in range(1, NX):
            arrived(xin.at[n, p - 1], us.at[n, p], ur.at[n, p], at(dx=1))
        for i in range(2):
            value = own[n, i] + (xin[n, 0, i].astype(F32) + xin[n, 1, i].astype(F32) + xin[n, 2, i].astype(F32))
            for j in range(QC):
                for lo in range(2):
                    part = value[j, :, lo * quarter:(lo + 1) * quarter]
                    if n == 0 and j == 0:
                        zown[lo, i] = part
                    zsend[n * QC + j, lo, i] = part.astype(BF16)
        for j in range(QC):
            q = n * QC + j
            if q == 0:
                send(zsend.at[0, 1 - z_lo], zin.at[0, z_lo], vs.at[0, 0], vr.at[0, z_lo], at(lo=1 - z_lo))
            else:
                for lo in range(2):
                    send(zsend.at[q, lo], zin.at[NQ - q, z_lo], vs.at[q, lo], vr.at[NQ - q, z_lo], at(dz=q, lo=lo))

    def last():
        total = [zown[z_lo, i] for i in range(2)]
        arrived(zin.at[0, 1 - z_lo], vs.at[0, 0], vr.at[0, 1 - z_lo], at(lo=1 - z_lo))
        for i in range(2):
            total[i] = total[i] + zin[0, 1 - z_lo, i].astype(F32)
        for q in range(1, NQ):
            for lo in range(2):
                arrived(zin.at[q, lo], vs.at[q, lo], vr.at[q, lo], at(dz=1, lo=lo))
                for i in range(2):
                    total[i] = total[i] + zin[q, lo, i].astype(F32)
        place = core * 2 + z_lo
        for i in range(2):
            fin[place, i] = total[i].astype(BF16)
        others = [(1 - z_lo, core), (z_lo, 1 - core), (1 - z_lo, 1 - core)]
        for n, (lo, k) in enumerate(others):
            send(fin.at[place], fin.at[place], fs.at[n], fr.at[n], at(lo=lo, k=k))
        for n, (lo, k) in enumerate(others):
            arrived(fin.at[k * 2 + lo], fs.at[n], fr.at[n], at(lo=lo, k=k))
        step = ROWS // 4
        for i, ref in enumerate((out_ref, back_ref)):
            for j in range(4):
                value = fin[j, i].astype(F32)
                pick = value[0:step]
                for k in range(1, 4):
                    pick = jnp.where(c == k, value[k * step:(k + 1) * step], pick)
                ref[:, j * quarter:(j + 1) * quarter] = pick.astype(BF16)

    order = [0, 1, 3, 2]
    for q in order:
        stage_x(q)
    for q in order[:QC]:
        stage_core(q)
    stage_mm(0)
    for q in order[QC:]:
        stage_core(q)
    stage_act(0)
    stage_mm(1)
    stores = []
    for h in range(2):
        for i in range(2):
            stores.append(pltpu.make_async_copy(tok.at[h, i], tok_out.at[i, (core + h) % 2], st_sem.at[h, i]))
    for store in stores:
        store.start()
    stage_out(0)
    stage_act(1)
    stage_z(0)
    stage_out(1)
    for n in range(NC):
        stores.append(pltpu.make_async_copy(act.at[n], act_out.at[n], st_sem.at[2, n]))
        stores[-1].start()
    stage_z(1)
    last()
    for copy in sends:
        copy.wait_send()
    for store in stores:
        store.wait()


def on_device(tokens_in, cotangent, w_gate, w_up, w_down):
    d, f = w_gate.shape
    half, quarter = d // 2, d // 4
    group = NX * ROWS
    share = QC * group // NY
    tokens = NQ * group
    dma = pltpu.SemaphoreType.DMA
    vmem = pl.BlockSpec(memory_space=pltpu.VMEM)
    anywhere = pl.BlockSpec(memory_space=pl.ANY)
    out, back, tok, act = pl.pallas_call(
        block_kernel,
        out_shape=[
            jax.ShapeDtypeStruct((4, d), BF16),
            jax.ShapeDtypeStruct((4, d), BF16),
            jax.ShapeDtypeStruct((2, 2, NQ, group, half), BF16),
            jax.ShapeDtypeStruct((NC, NY, 3, share, f), BF16),
        ],
        in_specs=[vmem, vmem, anywhere, anywhere, anywhere],
        out_specs=[vmem, vmem, anywhere, anywhere],
        scratch_shapes=[
            pltpu.VMEM((2, 2, NQ, group, half), BF16),
            pltpu.VMEM((2, half, f), BF16),
            pltpu.VMEM((2, half, f), BF16),
            pltpu.VMEM((2, f, half), BF16),
            pltpu.VMEM((NC, NY, 3, share, f), F32),
            pltpu.VMEM((NC, NY, 3, share, f), BF16),
            pltpu.VMEM((NC, NY - 1, 3, share, f), BF16),
            pltpu.VMEM((NC, NY, 3, share, f), BF16),
            pltpu.VMEM((NC, 2, QC * group, half), BF16),
            pltpu.VMEM((NC, 2, QC * group, half), BF16),
            pltpu.VMEM((NC, 2, QC, ROWS, half), F32),
            pltpu.VMEM((NC, NX - 1, 2, QC, ROWS, half), BF16),
            pltpu.VMEM((NC, NX - 1, 2, QC, ROWS, half), BF16),
            pltpu.VMEM((2, 2, ROWS, quarter), F32),
            pltpu.VMEM((NQ, 2, 2, ROWS, quarter), BF16),
            pltpu.VMEM((NQ, 2, 2, ROWS, quarter), BF16),
            pltpu.VMEM((4, 2, ROWS, quarter), BF16),
            dma((2, 3)),
            dma((3,)), dma((NQ,)),
            dma((NQ, NX)), dma((NQ, NX)),
            dma((NQ,)), dma((NQ,)),
            dma((NC, NY)), dma((NC, NY)),
            dma((NC, NY)), dma((NC, NY)),
            dma((NC,)), dma((NC,)),
            dma((NC, NX)), dma((NC, NX)),
            dma((NQ, 2)), dma((NQ, 2)),
            dma((3,)), dma((3,)),
            dma((3, 2)),
        ],
        compiler_params=pltpu.CompilerParams(
            collective_id=0, has_side_effects=True, vmem_limit_bytes=40 * 2**20
        ),
        cost_estimate=pl.CostEstimate(flops=12 * tokens * d * f, bytes_accessed=6 * d * f, transcendentals=tokens * f),
        name="block",
    )(tokens_in, cotangent, w_gate, w_up, w_down)
    tok = tok.reshape(2, 2, tokens, half)
    act = jnp.moveaxis(act, 2, 0).reshape(3, tokens, f)
    hidden, gate_back, up_back = act[0], act[1], act[2]
    tokens_full = jnp.concatenate([tok[0, 0], tok[0, 1]], axis=1)
    cotangent_full = jnp.concatenate([tok[1, 0], tok[1, 1]], axis=1)
    gate_grad = contract_first(tokens_full, gate_back).astype(BF16)
    up_grad = contract_first(tokens_full, up_back).astype(BF16)
    down_grad = contract_first(hidden, cotangent_full).astype(BF16)
    return (out, back, gate_grad, up_grad, down_grad)


def solution(mesh):
    return jax.shard_map(
        on_device,
        mesh=mesh,
        in_specs=(
            P("rows", "depth"),
            P("rows", "depth"),
            P("depth", ("rows", "cols")),
            P("depth", ("rows", "cols")),
            P(("rows", "cols"), "depth"),
        ),
        out_specs=(
            P(("rows", "cols"), "depth"),
            P(("rows", "cols"), "depth"),
            P("depth", ("rows", "cols")),
            P("depth", ("rows", "cols")),
            P(("rows", "cols"), "depth"),
        ),
        check_vma=False,
    )
```

```python
import functools

import jax
import jax.numpy as jnp
from jax import lax
from jax.experimental import pallas as pl
from jax.experimental.pallas import tpu as pltpu
from jax.sharding import PartitionSpec as P

MESH = pl.DeviceIdType.MESH
F32 = jnp.float32
BF16 = jnp.bfloat16
NQ = 4
NX = 4
NY = 4
NC = 2
QC = NQ // NC
ROWS = 16


def contract_last(left, right):
    return lax.dot_general(
        left, right, (((1,), (1,)), ((), ())), preferred_element_type=F32
    )


def matmul(left, right):
    return jnp.dot(left, right, preferred_element_type=F32)


def contract_first(left, right):
    return lax.dot_general(
        left, right, (((0,), (0,)), ((), ())), preferred_element_type=F32
    )


def block_kernel(
    tokens_ref, cot_ref, w_gate_ref, w_up_ref, w_down_ref,
    out_ref, back_ref, tok_out, act_out,
    tok, wg, wu, wd, part32, part16, part_in, act,
    core_send, core_in, own, xsend, xin, zown, zsend, zin, fin,
    load_sem, zs, zr, xs, xr, cs, cr, ys, yr, hs, hr, os_, or_, us, ur, vs, vr, fs, fr, st_sem,
):
    r, c, y = lax.axis_index("rows"), lax.axis_index("cols"), lax.axis_index("depth")
    z_hi, x = r // NX, r % NX
    z_lo, core = c // 2, c % 2
    half = tok.shape[-1]
    f = wg.shape[1]
    quarter = half // 2

    def at(dz=0, dx=0, lo=None, k=None, dy=0):
        lo = z_lo if lo is None else lo
        k = core if k is None else k
        row = lax.rem(z_hi + dz, NQ) * NX + lax.rem(x + dx, NX)
        return (row, lo * 2 + k, lax.rem(y + dy, NY))

    loads = []
    for h in range(2):
        place = pl.multiple_of((core + h) % 2 * half, half)
        loads.append([
            pltpu.make_async_copy(ref.at[:, pl.ds(place, half)], held.at[h], load_sem.at[h, i])
            for i, (ref, held) in enumerate(((w_gate_ref, wg), (w_up_ref, wu), (w_down_ref, wd)))
        ])
    for group in loads:
        for load in group:
            load.start()

    barrier = pltpu.get_barrier_semaphore()
    partners = [at(dx=d) for d in range(1, NX)] + [at(dy=d) for d in range(1, NY)]
    partners += [at(dz=d, lo=lo) for d in range(1, NQ) for lo in range(2)]
    partners += [at(lo=1 - z_lo), at(k=1 - core), at(lo=1 - z_lo, k=1 - core)]
    for partner in partners:
        pl.semaphore_signal(barrier, inc=1, device_id=partner, device_id_type=MESH)

    mine = pl.ds(pl.multiple_of(core * half, half), half)
    tok[0, 0, 0, 0:ROWS] = tokens_ref[:, mine]
    tok[0, 1, 0, 0:ROWS] = cot_ref[:, mine]
    pl.semaphore_wait(barrier, len(partners))

    sends = []

    def send(src, dst, ss, rs, to):
        copy = pltpu.make_async_remote_copy(
            src_ref=src, dst_ref=dst, send_sem=ss, recv_sem=rs, device_id=to, device_id_type=MESH
        )
        copy.start()
        sends.append(copy)

    def arrived(dst, ss, rs, to):
        pltpu.make_async_remote_copy(
            src_ref=dst, dst_ref=dst, send_sem=ss, recv_sem=rs, device_id=to, device_id_type=MESH
        ).wait_recv()

    shift = 1 + 2 * (1 - z_lo)
    slot = 4 - shift
    own_shard = tok.at[0, :, 0, pl.ds(0, ROWS)]
    for lo in range(2):
        send(own_shard, tok.at[0, :, slot, pl.ds(0, ROWS)], zs.at[lo], zr.at[slot], at(dz=shift, lo=lo))
    send(own_shard, tok.at[0, :, 2, pl.ds(0, ROWS)], zs.at[2], zr.at[2], at(dz=2, lo=1 - z_lo))

    def stage_x(q):
        if q:
            arrived(tok.at[0, :, q, pl.ds(0, ROWS)], zs.at[0], zr.at[q], at(dx=1))
        for d in range(1, NX):
            p = NX - d
            send(
                tok.at[0, :, q, pl.ds(0, ROWS)], tok.at[0, :, q, pl.ds(p * ROWS, ROWS)],
                xs.at[q, d], xr.at[q, p], at(dx=d),
            )

    def stage_core(q):
        for p in range(1, NX):
            arrived(tok.at[0, :, q, pl.ds(p * ROWS, ROWS)], xs.at[q, p], xr.at[q, p], at(dx=1))
        send(tok.at[0, :, q], tok.at[1, :, q], cs.at[q], cr.at[q], at(k=1 - core))

    rows = QC * NX * ROWS
    share = rows // NY

    def stage_mm(n):
        gs = pl.ds(n * QC, QC)
        sums = []
        for h in range(2):
            if n == 0:
                for load in loads[h]:
                    load.wait()
            if h:
                for q in range(n * QC, n * QC + QC):
                    arrived(tok.at[1, :, q], cs.at[q], cr.at[q], at(k=1 - core))
            t = tok[h, 0, gs].reshape(rows, half)
            g = tok[h, 1, gs].reshape(rows, half)
            terms = [
                contract_last(t, wg[h]),
                contract_last(t, wu[h]),
                contract_last(g, wd[h]),
            ]
            for i, term in enumerate(terms):
                term = term.reshape(NY, share, f)
                if h:
                    term = term + part32[n, :, i]
                    part16[n, :, i] = term.astype(BF16)
                part32[n, :, i] = term
        for d in range(1, NY):
            to = lax.rem(y + d, NY)
            send(part16.at[n, to], part_in.at[n, NY - d - 1], ys.at[n, d], yr.at[n, NY - d], at(dy=d))

    def stage_act(n):
        for p in range(1, NY):
            arrived(part_in.at[n, p - 1], ys.at[n, p], yr.at[n, p], at(dy=1))
        gate, up, hidden_back = [
            part32[n, y, i] + (part_in[n, 0, i].astype(F32) + part_in[n, 1, i].astype(F32)
                               + part_in[n, 2, i].astype(F32))
            for i in range(3)
        ]
        sigma = jax.nn.sigmoid(gate)
        act[n, y, 0] = (gate * sigma * up).astype(BF16)
        act[n, y, 1] = (hidden_back * up * sigma * (1.0 + gate * (1.0 - sigma))).astype(BF16)
        act[n, y, 2] = (hidden_back * gate * sigma).astype(BF16)
        for d in range(1, NY):
            send(act.at[n, y], act.at[n, y], hs.at[n, d], hr.at[n, NY - d], at(dy=d))

    def stage_out(n):
        for p in range(1, NY):
            arrived(act.at[n, lax.rem(y + p, NY)], hs.at[n, p], hr.at[n, p], at(dy=1))
        hidden, gate_back, up_back = [act[n, :, i].reshape(rows, f) for i in range(3)]

        def outputs(h):
            return [
                matmul(hidden, wd[h]),
                matmul(gate_back, wg[h]) + matmul(up_back, wu[h]),
            ]

        for i, value in enumerate(outputs(1)):
            core_send[n, i] = value.astype(core_send.dtype)
        send(core_send.at[n], core_in.at[n], os_.at[n], or_.at[n], at(k=1 - core))
        values = outputs(0)
        arrived(core_in.at[n], os_.at[n], or_.at[n], at(k=1 - core))
        for i, value in enumerate(values):
            value = (value + core_in[n, i].astype(F32)).reshape(QC, NX, ROWS, half)
            own[n, i] = value[:, 0]
            for p in range(1, NX):
                xsend[n, p - 1, i] = value[:, p].astype(BF16)
        for d in range(1, NX):
            send(xsend.at[n, d - 1], xin.at[n, NX - d - 1], us.at[n, d], ur.at[n, NX - d], at(dx=d))

    def stage_z(n):
        for p in range(1, NX):
            arrived(xin.at[n, p - 1], us.at[n, p], ur.at[n, p], at(dx=1))
        for i in range(2):
            value = own[n, i] + (xin[n, 0, i].astype(F32) + xin[n, 1, i].astype(F32) + xin[n, 2, i].astype(F32))
            for j in range(QC):
                for lo in range(2):
                    part = value[j, :, lo * quarter:(lo + 1) * quarter]
                    if n == 0 and j == 0:
                        zown[lo, i] = part
                    zsend[n * QC + j, lo, i] = part.astype(BF16)
        for j in range(QC):
            q = n * QC + j
            if q == 0:
                send(zsend.at[0, 1 - z_lo], zin.at[0, z_lo], vs.at[0, 0], vr.at[0, z_lo], at(lo=1 - z_lo))
            else:
                for lo in range(2):
                    send(zsend.at[q, lo], zin.at[NQ - q, z_lo], vs.at[q, lo], vr.at[NQ - q, z_lo], at(dz=q, lo=lo))

    def last():
        total = [zown[z_lo, i] for i in range(2)]
        arrived(zin.at[0, 1 - z_lo], vs.at[0, 0], vr.at[0, 1 - z_lo], at(lo=1 - z_lo))
        for i in range(2):
            total[i] = total[i] + zin[0, 1 - z_lo, i].astype(F32)
        for q in range(1, NQ):
            for lo in range(2):
                arrived(zin.at[q, lo], vs.at[q, lo], vr.at[q, lo], at(dz=1, lo=lo))
                for i in range(2):
                    total[i] = total[i] + zin[q, lo, i].astype(F32)
        place = core * 2 + z_lo
        for i in range(2):
            fin[place, i] = total[i].astype(BF16)
        others = [(1 - z_lo, core), (z_lo, 1 - core), (1 - z_lo, 1 - core)]
        for n, (lo, k) in enumerate(others):
            send(fin.at[place], fin.at[place], fs.at[n], fr.at[n], at(lo=lo, k=k))
        for n, (lo, k) in enumerate(others):
            arrived(fin.at[k * 2 + lo], fs.at[n], fr.at[n], at(lo=lo, k=k))
        step = ROWS // 4
        for i, ref in enumerate((out_ref, back_ref)):
            for j in range(4):
                value = fin[j, i].astype(F32)
                pick = value[0:step]
                for k in range(1, 4):
                    pick = jnp.where(c == k, value[k * step:(k + 1) * step], pick)
                ref[:, j * quarter:(j + 1) * quarter] = pick.astype(BF16)

    order = [0, 1, 3, 2]
    for q in order:
        stage_x(q)
    for q in order[:QC]:
        stage_core(q)
    stage_mm(0)
    for q in order[QC:]:
        stage_core(q)
    stage_act(0)
    stage_mm(1)
    stores = []
    for h in range(2):
        for i in range(2):
            place = pl.ds(pl.multiple_of((core + h) % 2 * half, half), half)
            stores.append(pltpu.make_async_copy(tok.at[h, i], tok_out.at[i, :, :, place], st_sem.at[h, i]))
    for store in stores:
        store.start()
    stage_out(0)
    stage_act(1)
    stage_z(0)
    stage_out(1)
    for n in range(NC):
        for i in range(3):
            stores.append(pltpu.make_async_copy(act.at[n, :, i], act_out.at[i, n], st_sem.at[2 + n, i]))
            stores[-1].start()
    stage_z(1)
    last()
    for copy in sends:
        copy.wait_send()
    for store in stores:
        store.wait()


def grads_kernel(out_ref, back_ref, tok_ref, act_ref, out_copy, back_copy, gate_grad, up_grad, down_grad):
    @pl.when(pl.program_id(0) == 0)
    def _():
        out_copy[...] = out_ref[...]
        back_copy[...] = back_ref[...]

    f = act_ref.shape[-1]
    tokens, cot = [tok_ref[i].reshape(-1, tok_ref.shape[-1]) for i in range(2)]
    hidden, gate_back, up_back = [act_ref[i].reshape(-1, f) for i in range(3)]
    gate_grad[...] = contract_first(gate_back, tokens).astype(BF16)
    up_grad[...] = contract_first(up_back, tokens).astype(BF16)
    down_grad[...] = contract_first(hidden, cot).astype(BF16)


def weight_grads(out, back, tok, act):
    d, f = tok.shape[-1], act.shape[-1]
    tile = 512
    whole = pl.BlockSpec(out.shape, lambda i: (0, 0))
    grad = pl.BlockSpec((f, tile), lambda i: (0, i))
    small = jax.ShapeDtypeStruct(out.shape, BF16)
    large = jax.ShapeDtypeStruct((f, d), BF16)
    return pl.pallas_call(
        grads_kernel,
        grid=(d // tile,),
        out_shape=[small, small, large, large, large],
        in_specs=[
            whole, whole,
            pl.BlockSpec(tok.shape[:-1] + (tile,), lambda i: (0,) * (tok.ndim - 1) + (i,)),
            pl.BlockSpec(act.shape, lambda i: (0,) * act.ndim),
        ],
        out_specs=[whole, whole, grad, grad, grad],
        compiler_params=pltpu.CompilerParams(vmem_limit_bytes=56 * 2**20),
        name="grads",
    )(out, back, tok, act)


def on_device(tokens_in, cotangent, w_gate, w_up, w_down):
    d, f = w_gate.shape
    half, quarter = d // 2, d // 4
    group = NX * ROWS
    share = QC * group // NY
    tokens = NQ * group
    dma = pltpu.SemaphoreType.DMA
    vmem = pl.BlockSpec(memory_space=pltpu.VMEM)
    anywhere = pl.BlockSpec(memory_space=pl.ANY)
    hbm = pl.BlockSpec(memory_space=pltpu.HBM)
    out, back, tok, act = pl.pallas_call(
        block_kernel,
        out_shape=[
            jax.ShapeDtypeStruct((4, d), BF16),
            jax.ShapeDtypeStruct((4, d), BF16),
            jax.ShapeDtypeStruct((2, NQ, group, d), BF16),
            jax.ShapeDtypeStruct((3, NC, NY, share, f), BF16),
        ],
        in_specs=[vmem, vmem, hbm, hbm, hbm],
        out_specs=[vmem, vmem, anywhere, anywhere],
        scratch_shapes=[
            pltpu.VMEM((2, 2, NQ, group, half), BF16),
            pltpu.VMEM((2, f, half), BF16),
            pltpu.VMEM((2, f, half), BF16),
            pltpu.VMEM((2, f, half), BF16),
            pltpu.VMEM((NC, NY, 3, share, f), F32),
            pltpu.VMEM((NC, NY, 3, share, f), BF16),
            pltpu.VMEM((NC, NY - 1, 3, share, f), BF16),
            pltpu.VMEM((NC, NY, 3, share, f), BF16),
            pltpu.VMEM((NC, 2, QC * group, half), BF16),
            pltpu.VMEM((NC, 2, QC * group, half), BF16),
            pltpu.VMEM((NC, 2, QC, ROWS, half), F32),
            pltpu.VMEM((NC, NX - 1, 2, QC, ROWS, half), BF16),
            pltpu.VMEM((NC, NX - 1, 2, QC, ROWS, half), BF16),
            pltpu.VMEM((2, 2, ROWS, quarter), F32),
            pltpu.VMEM((NQ, 2, 2, ROWS, quarter), BF16),
            pltpu.VMEM((NQ, 2, 2, ROWS, quarter), BF16),
            pltpu.VMEM((4, 2, ROWS, quarter), BF16),
            dma((2, 3)),
            dma((3,)), dma((NQ,)),
            dma((NQ, NX)), dma((NQ, NX)),
            dma((NQ,)), dma((NQ,)),
            dma((NC, NY)), dma((NC, NY)),
            dma((NC, NY)), dma((NC, NY)),
            dma((NC,)), dma((NC,)),
            dma((NC, NX)), dma((NC, NX)),
            dma((NQ, 2)), dma((NQ, 2)),
            dma((3,)), dma((3,)),
            dma((2 + NC, 3)),
        ],
        compiler_params=pltpu.CompilerParams(
            collective_id=0, has_side_effects=True, vmem_limit_bytes=56 * 2**20
        ),
        cost_estimate=pl.CostEstimate(flops=12 * tokens * d * f, bytes_accessed=6 * d * f, transcendentals=tokens * f),
        name="block",
    )(tokens_in, cotangent, w_gate.T, w_up.T, w_down)
    out, back, gate_grad, up_grad, down_grad = weight_grads(out, back, tok, act)
    return (out, back, gate_grad.T, up_grad.T, down_grad)


def solution(mesh):
    return jax.shard_map(
        on_device,
        mesh=mesh,
        in_specs=(
            P("rows", "depth"),
            P("rows", "depth"),
            P("depth", ("rows", "cols")),
            P("depth", ("rows", "cols")),
            P(("rows", "cols"), "depth"),
        ),
        out_specs=(
            P(("rows", "cols"), "depth"),
            P(("rows", "cols"), "depth"),
            P("depth", ("rows", "cols")),
            P("depth", ("rows", "cols")),
            P(("rows", "cols"), "depth"),
        ),
        check_vma=False,
    )
```

```python
import functools

import jax
import jax.numpy as jnp
from jax import lax
from jax.experimental import pallas as pl
from jax.experimental.pallas import tpu as pltpu
from jax.sharding import PartitionSpec as P

MESH = pl.DeviceIdType.MESH
F32 = jnp.float32
BF16 = jnp.bfloat16
NQ = 4
NX = 4
NY = 4
ORDER = [0, 1, 3, 2]
ROWS = 16


def contract_last(left, right):
    return lax.dot_general(
        left, right, (((1,), (1,)), ((), ())), preferred_element_type=F32
    )


def matmul(left, right):
    return jnp.dot(left, right, preferred_element_type=F32)


def contract_first(left, right):
    return lax.dot_general(
        left, right, (((0,), (0,)), ((), ())), preferred_element_type=F32
    )


def block_kernel(
    tokens_ref, cot_ref, w_gate_ref, w_up_ref, w_down_ref,
    out_ref, back_ref, tok_out, act_out,
    tok, held, other, part32, part16, part_in, act, act_other,
    own, xsend, xin, zf, zsend, zin,
    load_sem, ws, wr, zs, zr, xs, xr, fs, fr, cs, cr, ys, yr, hs, hr, ks, kr, us, ur, vs, vr, st_sem,
):
    r, c, y = lax.axis_index("rows"), lax.axis_index("cols"), lax.axis_index("depth")
    z_hi, x = r // NX, r % NX
    z_lo, core = c // 2, c % 2
    half = tok.shape[-1]
    f = held.shape[2]
    piece = half // 4
    weights = (w_gate_ref, w_up_ref, w_down_ref)

    def at(dz=0, dx=0, lo=None, k=None, dy=0):
        lo = z_lo if lo is None else lo
        k = core if k is None else k
        row = lax.rem(z_hi + dz, NQ) * NX + lax.rem(x + dx, NX)
        return (row, lo * 2 + k, lax.rem(y + dy, NY))

    def features(h):
        return pl.ds(pl.multiple_of((core + h) % 2 * half, half), half)

    loads = [
        [
            pltpu.make_async_copy(ref.at[:, features(h)], held.at[h, i], load_sem.at[h, i])
            for i, ref in enumerate(weights)
        ]
        for h in range(2)
    ]
    for group in loads:
        for load in group:
            load.start()

    barrier = pltpu.get_barrier_semaphore()
    neighbour = at(k=1 - core)
    group = [(1 - z_lo, core), (z_lo, 1 - core), (1 - z_lo, 1 - core)]
    partners = [at(dx=d) for d in range(1, NX)] + [at(dy=d) for d in range(1, NY)]
    partners += [at(dz=d, lo=lo, k=k) for d in range(1, NQ) for lo in range(2) for k in range(2)]
    partners += [at(lo=lo, k=k) for lo, k in group]
    for partner in partners:
        pl.semaphore_signal(barrier, inc=1, device_id=partner, device_id_type=MESH)

    tok[0, 0, 0, 0:ROWS] = tokens_ref[:, features(0)]
    tok[0, 1, 0, 0:ROWS] = cot_ref[:, features(0)]
    pl.semaphore_wait(barrier, len(partners))

    sends = []

    def send(src, dst, ss, rs, to):
        copy = pltpu.make_async_remote_copy(
            src_ref=src, dst_ref=dst, send_sem=ss, recv_sem=rs, device_id=to, device_id_type=MESH
        )
        copy.start()
        sends.append(copy)

    def arrived(dst, ss, rs):
        pltpu.make_async_remote_copy(
            src_ref=dst, dst_ref=dst, send_sem=ss, recv_sem=rs, device_id=neighbour, device_id_type=MESH
        ).wait_recv()

    def shard(q, p):
        return tok.at[0, :, q, pl.ds(p * ROWS, ROWS)]

    shift = 1 + 2 * (1 - z_lo)
    slot = 4 - shift

    def stage_x(q):
        if q:
            arrived(shard(q, 0), zs.at[0], zr.at[q])
        for d in (1, NX - 1):
            send(shard(q, 0), shard(q, NX - d), xs.at[q, d], xr.at[q, NX - d], at(dx=d))

    def stage_pass(q):
        for i, p in enumerate((NX - 1, 1)):
            arrived(shard(q, p), xs.at[q, p], xr.at[q, p])
            send(
                tok.at[0, i, q, pl.ds(p * ROWS, ROWS)], tok.at[0, i, q, pl.ds(2 * ROWS, ROWS)],
                fs.at[q, i], fr.at[q, i], at(dx=NX - p),
            )

    def stage_core(q):
        for i in range(2):
            arrived(tok.at[0, i, q, pl.ds(2 * ROWS, ROWS)], fs.at[q, i], fr.at[q, i])
        send(tok.at[0, :, q], tok.at[1, :, q], cs.at[q], cr.at[q], neighbour)

    def stage_weight(i):
        send(weights[i].at[:, features(1)], other.at[i], ws.at[i], wr.at[i], neighbour)

    rows = NX * ROWS
    share = rows // NY

    def stage_mm(n):
        for h in range(2):
            if n == 0:
                for load in loads[h]:
                    load.wait()
            if h:
                arrived(tok.at[1, :, n], cs.at[n], cr.at[n])
            for i in range(3):
                term = contract_last(tok[h, i // 2, n], held[h, i]).reshape(NY, share, f)
                if h:
                    term = term + part32[n, :, i]
                    part16[n, :, i] = term.astype(BF16)
                part32[n, :, i] = term
        for d in (1, 3, 2):
            to = lax.rem(y + d, NY)
            send(part16.at[n, to], part_in.at[n, NY - d - 1], ys.at[n, d], yr.at[n, NY - d], at(dy=d))

    def stage_act(n):
        for p in range(1, NY):
            arrived(part_in.at[n, p - 1], ys.at[n, p], yr.at[n, p])
        gate, up, hidden_back = [
            part32[n, y, i] + (part_in[n, 0, i].astype(F32) + part_in[n, 1, i].astype(F32)
                               + part_in[n, 2, i].astype(F32))
            for i in range(3)
        ]
        sigma = jax.nn.sigmoid(gate)
        act[n, y, 0] = (gate * sigma * up).astype(BF16)
        act[n, y, 1] = (hidden_back * up * sigma * (1.0 + gate * (1.0 - sigma))).astype(BF16)
        act[n, y, 2] = (hidden_back * gate * sigma).astype(BF16)
        for d in (1, 3, 2):
            send(act.at[n, y], act.at[n, y], hs.at[n, d], hr.at[n, NY - d], at(dy=d))
        send(act.at[n, y], act_other.at[n, y], ks.at[n, 0], kr.at[n, 0], neighbour)

    def stage_out(n):
        for p in (1, 3, 2):
            place = lax.rem(y + p, NY)
            arrived(act.at[n, place], hs.at[n, p], hr.at[n, p])
            send(act.at[n, place], act_other.at[n, place], ks.at[n, p], kr.at[n, p], neighbour)

        def outputs(ref, w):
            hidden, gate_back, up_back = [ref[n, :, i].reshape(rows, f) for i in range(3)]
            return [matmul(hidden, w[2]), matmul(gate_back, w[0]) + matmul(up_back, w[1])]

        mine = outputs(act, held.at[0])
        if n == 0:
            for i in range(3):
                arrived(other.at[i], ws.at[i], wr.at[i])
        for p in range(NY):
            arrived(act_other.at[n, lax.rem(y + p, NY)], ks.at[n, p], kr.at[n, p])
        for i, (left, right) in enumerate(zip(mine, outputs(act_other, other))):
            value = (left + right).reshape(NX, ROWS, half)
            own[n, i] = value[0]
            for p in range(1, NX):
                xsend[n, p - 1, i] = value[p].astype(BF16)
        for d in (1, 3, 2):
            send(xsend.at[n, d - 1], xin.at[n, NX - d - 1], us.at[n, d], ur.at[n, NX - d], at(dx=d))

    def stage_z(n):
        for p in range(1, NX):
            arrived(xin.at[n, p - 1], us.at[n, p], ur.at[n, p])
        step = ROWS // 4
        for i in range(2):
            value = own[n, i] + (xin[n, 0, i].astype(F32) + xin[n, 1, i].astype(F32) + xin[n, 2, i].astype(F32))
            for k in range(4):
                for j in range(4):
                    zf[n, k, i, j * step:(j + 1) * step] = value[k * step:(k + 1) * step, j * piece:(j + 1) * piece]
                zsend[n, k, i] = zf[n, k, i].astype(BF16)
        back = (NQ - n) % NQ
        for lo, k in group if n == 0 else [(0, 0), (0, 1), (1, 0), (1, 1)]:
            to = lo * 2 + k
            send(zsend.at[n, to], zin.at[back, c], vs.at[n, to], vr.at[back, c], at(dz=n, lo=lo, k=k))

    def last():
        zin[0, c] = zsend[0, c]
        sums = [[None, None], [None, None]]
        for lo, k in group:
            to = lo * 2 + k
            arrived(zin.at[0, to], vs.at[0, to], vr.at[0, to])
        for q in ORDER:
            for to in range(4):
                if q:
                    arrived(zin.at[q, to], vs.at[q, to], vr.at[q, to])
                for i in range(2):
                    value = zin[q, to, i].astype(F32)
                    if q == 0:
                        value = jnp.where(c == to, zf[0, to, i], value)
                    total = sums[to % 2][i]
                    sums[to % 2][i] = value if total is None else total + value
        step = ROWS // 4
        for i, ref in enumerate((out_ref, back_ref)):
            for k in range(2):
                for j in range(4):
                    ref[:, k * half + j * piece:k * half + (j + 1) * piece] = (
                        sums[k][i][j * step:(j + 1) * step].astype(BF16)
                    )

    stores = []

    def store_tokens():
        for h in range(2):
            for i in range(2):
                stores.append(pltpu.make_async_copy(tok.at[h, i], tok_out.at[i, :, :, features(h)], st_sem.at[h, i]))
                stores[-1].start()

    def store_act(n):
        for i in range(3):
            stores.append(pltpu.make_async_copy(act.at[n, :, i], act_out.at[i, n], st_sem.at[2 + n, i]))
            stores[-1].start()

    for lo in range(2):
        send(shard(0, 0), shard(slot, 0), zs.at[lo], zr.at[slot], at(dz=shift, lo=lo))
    send(shard(0, 0), shard(2, 0), zs.at[2], zr.at[2], at(dz=2, lo=1 - z_lo))
    stage_x(0)
    stage_x(1)
    stage_x(3)
    stage_pass(0)
    stage_x(2)
    stage_pass(1)
    stage_core(0)
    stage_pass(3)
    stage_mm(0)
    stage_pass(2)
    stage_core(1)
    stage_weight(0)
    stage_core(3)
    stage_weight(1)
    stage_mm(1)
    stage_act(0)
    stage_core(2)
    stage_weight(2)
    stage_mm(3)
    stage_act(1)
    stage_mm(2)
    store_tokens()
    stage_out(0)
    stage_act(3)
    stage_out(1)
    stage_act(2)
    stage_z(0)
    stage_out(3)
    stage_z(1)
    stage_out(2)
    for n in ORDER:
        store_act(n)
    stage_z(3)
    stage_z(2)
    last()
    for copy in sends:
        copy.wait_send()
    for store in stores:
        store.wait()


def grads_kernel(out_ref, back_ref, tok_ref, act_ref, out_copy, back_copy, gate_grad, up_grad, down_grad):
    @pl.when(pl.program_id(0) == 0)
    def _():
        out_copy[...] = out_ref[...]
        back_copy[...] = back_ref[...]

    f = act_ref.shape[-1]
    tokens, cot = [tok_ref[i].reshape(-1, tok_ref.shape[-1]) for i in range(2)]
    hidden, gate_back, up_back = [act_ref[i].reshape(-1, f) for i in range(3)]
    gate_grad[...] = contract_first(gate_back, tokens).astype(BF16)
    up_grad[...] = contract_first(up_back, tokens).astype(BF16)
    down_grad[...] = contract_first(hidden, cot).astype(BF16)


def weight_grads(out, back, tok, act):
    d, f = tok.shape[-1], act.shape[-1]
    tile = 512
    whole = pl.BlockSpec(out.shape, lambda i: (0, 0))
    grad = pl.BlockSpec((f, tile), lambda i: (0, i))
    small = jax.ShapeDtypeStruct(out.shape, BF16)
    large = jax.ShapeDtypeStruct((f, d), BF16)
    return pl.pallas_call(
        grads_kernel,
        grid=(d // tile,),
        out_shape=[small, small, large, large, large],
        in_specs=[
            whole, whole,
            pl.BlockSpec(tok.shape[:-1] + (tile,), lambda i: (0,) * (tok.ndim - 1) + (i,)),
            pl.BlockSpec(act.shape, lambda i: (0,) * act.ndim),
        ],
        out_specs=[whole, whole, grad, grad, grad],
        compiler_params=pltpu.CompilerParams(vmem_limit_bytes=56 * 2**20),
        name="grads",
    )(out, back, tok, act)


def on_device(tokens_in, cotangent, w_gate, w_up, w_down):
    d, f = w_gate.shape
    half = d // 2
    piece = half // 4
    group = NX * ROWS
    share = group // NY
    tokens = NQ * group
    dma = pltpu.SemaphoreType.DMA
    vmem = pl.BlockSpec(memory_space=pltpu.VMEM)
    hbm = pl.BlockSpec(memory_space=pltpu.HBM)
    out, back, tok, act = pl.pallas_call(
        block_kernel,
        out_shape=[
            jax.ShapeDtypeStruct((4, d), BF16),
            jax.ShapeDtypeStruct((4, d), BF16),
            jax.ShapeDtypeStruct((2, NQ, group, d), BF16),
            jax.ShapeDtypeStruct((3, NQ, NY, share, f), BF16),
        ],
        in_specs=[vmem, vmem, hbm, hbm, hbm],
        out_specs=[vmem, vmem, hbm, hbm],
        scratch_shapes=[
            pltpu.VMEM((2, 2, NQ, group, half), BF16),
            pltpu.VMEM((2, 3, f, half), BF16),
            pltpu.VMEM((3, f, half), BF16),
            pltpu.VMEM((NQ, NY, 3, share, f), F32),
            pltpu.VMEM((NQ, NY, 3, share, f), BF16),
            pltpu.VMEM((NQ, NY - 1, 3, share, f), BF16),
            pltpu.VMEM((NQ, NY, 3, share, f), BF16),
            pltpu.VMEM((NQ, NY, 3, share, f), BF16),
            pltpu.VMEM((NQ, 2, ROWS, half), F32),
            pltpu.VMEM((NQ, NX - 1, 2, ROWS, half), BF16),
            pltpu.VMEM((NQ, NX - 1, 2, ROWS, half), BF16),
            pltpu.VMEM((NQ, 4, 2, ROWS, piece), F32),
            pltpu.VMEM((NQ, 4, 2, ROWS, piece), BF16),
            pltpu.VMEM((NQ, 4, 2, ROWS, piece), BF16),
            dma((2, 3)),
            dma((3,)), dma((3,)),
            dma((3,)), dma((NQ,)),
            dma((NQ, NX)), dma((NQ, NX)),
            dma((NQ, 2)), dma((NQ, 2)),
            dma((NQ,)), dma((NQ,)),
            dma((NQ, NY)), dma((NQ, NY)),
            dma((NQ, NY)), dma((NQ, NY)),
            dma((NQ, NY)), dma((NQ, NY)),
            dma((NQ, NX)), dma((NQ, NX)),
            dma((NQ, 4)), dma((NQ, 4)),
            dma((2 + NQ, 3)),
        ],
        compiler_params=pltpu.CompilerParams(
            collective_id=0, has_side_effects=True, vmem_limit_bytes=56 * 2**20
        ),
        cost_estimate=pl.CostEstimate(flops=12 * tokens * d * f, bytes_accessed=6 * d * f, transcendentals=tokens * f),
        name="block",
    )(tokens_in, cotangent, w_gate.T, w_up.T, w_down)
    out, back, gate_grad, up_grad, down_grad = weight_grads(out, back, tok, act)
    return (out, back, gate_grad.T, up_grad.T, down_grad)


def solution(mesh):
    return jax.shard_map(
        on_device,
        mesh=mesh,
        in_specs=(
            P("rows", "depth"),
            P("rows", "depth"),
            P("depth", ("rows", "cols")),
            P("depth", ("rows", "cols")),
            P(("rows", "cols"), "depth"),
        ),
        out_specs=(
            P(("rows", "cols"), "depth"),
            P(("rows", "cols"), "depth"),
            P("depth", ("rows", "cols")),
            P("depth", ("rows", "cols")),
            P(("rows", "cols"), "depth"),
        ),
        check_vma=False,
    )
```

```python
import functools

import jax
import jax.numpy as jnp
from jax import lax
from jax.experimental import pallas as pl
from jax.experimental.pallas import tpu as pltpu
from jax.sharding import PartitionSpec as P

MESH = pl.DeviceIdType.MESH
F32 = jnp.float32
BF16 = jnp.bfloat16
NQ = 4
NX = 4
NY = 4
ORDER = [0, 1, 3, 2]
ROWS = 16


def contract_last(left, right):
    return lax.dot_general(
        left, right, (((1,), (1,)), ((), ())), preferred_element_type=F32
    )


def matmul(left, right):
    return jnp.dot(left, right, preferred_element_type=F32)


def contract_first(left, right):
    return lax.dot_general(
        left, right, (((0,), (0,)), ((), ())), preferred_element_type=F32
    )


def block_kernel(
    tokens_ref, cot_ref, w_gate_ref, w_up_ref, w_down_ref,
    out_ref, back_ref, tok_out, act_out,
    tok, held, other, part32, part16, part_in, act, act_other,
    own, xsend, xin, zf, zsend, zin,
    load_sem, store_sem, sent, wr, zr, xr, cr, yr, hr, kr, ur, vr,
):
    r, c, y = lax.axis_index("rows"), lax.axis_index("cols"), lax.axis_index("depth")
    z_hi, x = r // NX, r % NX
    z_lo, core = c // 2, c % 2
    half = tok.shape[-1]
    f = held.shape[2]
    piece = half // 4
    weights = (w_gate_ref, w_up_ref, w_down_ref)

    def at(dz=0, dx=0, lo=None, k=None, dy=0):
        lo = z_lo if lo is None else lo
        k = core if k is None else k
        row = lax.rem(z_hi + dz, NQ) * NX + lax.rem(x + dx, NX)
        return (row, lo * 2 + k, lax.rem(y + dy, NY))

    def features(h):
        return pl.ds(pl.multiple_of((core + h) % 2 * half, half), half)

    for h in range(2):
        for i, ref in enumerate(weights):
            pltpu.make_async_copy(ref.at[:, features(h)], held.at[h, i], load_sem.at[h]).start()

    barrier = pltpu.get_barrier_semaphore()
    neighbour = at(k=1 - core)
    group = [(1 - z_lo, core), (z_lo, 1 - core), (1 - z_lo, 1 - core)]
    partners = [at(dx=d) for d in range(1, NX)] + [at(dy=d) for d in range(1, NY)]
    partners += [at(dz=d, lo=lo, k=k) for d in range(1, NQ) for lo in range(2) for k in range(2)]
    partners += [at(lo=lo, k=k) for lo, k in group]
    for partner in partners:
        pl.semaphore_signal(barrier, inc=1, device_id=partner, device_id_type=MESH)

    tok[0, 0, 0, 0:ROWS] = tokens_ref[:, features(0)]
    tok[0, 1, 0, 0:ROWS] = cot_ref[:, features(0)]
    pl.semaphore_wait(barrier, len(partners))

    Z, X, CORE, WEIGHT, SUM, ACT, PASS, OUT, NEAR, FAR = range(10)

    def send(src, dst, kind, rs, to):
        pltpu.make_async_remote_copy(
            src_ref=src, dst_ref=dst, send_sem=sent.at[kind], recv_sem=rs, device_id=to, device_id_type=MESH
        ).start()

    def arrived(dst, rs):
        pltpu.make_async_remote_copy(
            src_ref=dst, dst_ref=dst, send_sem=sent.at[0], recv_sem=rs, device_id=neighbour, device_id_type=MESH
        ).wait_recv()

    def left(size, kind):
        pltpu.make_async_remote_copy(
            src_ref=size, dst_ref=size, send_sem=sent.at[kind], recv_sem=wr.at[0], device_id=neighbour, device_id_type=MESH
        ).wait_send()

    def shard(q, p):
        return tok.at[0, :, q, pl.ds(p * ROWS, ROWS)]

    shift = 1 + 2 * (1 - z_lo)
    slot = 4 - shift

    PASSED = (1, 3)

    def stage_x(q):
        if q:
            arrived(shard(q, 0), zr.at[q])
        for d in (1, 3) if q in PASSED else (1, 3, 2):
            p = NX - d
            send(shard(q, 0), shard(q, p), X, xr.at[q, p if q in PASSED else 0], at(dx=d))

    def stage_pass(q):
        for i, p in enumerate((NX - 1, 1)):
            arrived(shard(q, p), xr.at[q, p])
            here = tok.at[0, i, q, pl.ds(p * ROWS, ROWS)]
            there = tok.at[0, i, q, pl.ds(2 * ROWS, ROWS)]
            send(here, there, X, xr.at[q, 2], at(dx=NX - p))

    def stage_core(q):
        if q in PASSED:
            arrived(shard(q, 2), xr.at[q, 2])
        else:
            arrived(tok.at[0, :, q, pl.ds(ROWS, 3 * ROWS)], xr.at[q, 0])
        send(tok.at[0, :, q], tok.at[1, :, q], CORE, cr.at[q], neighbour)

    def stage_weight(i):
        send(weights[i].at[:, features(1)], other.at[i], WEIGHT, wr.at[0], neighbour)

    rows = NX * ROWS
    share = rows // NY

    def stage_mm(n, h):
        if n == 0:
            pltpu.make_async_copy(held.at[h], held.at[h], load_sem.at[h]).wait()
        if h:
            arrived(tok.at[1, :, n], cr.at[n])
        both = contract_last(tok[h, 0, n], held[h, 0:2].reshape(2 * f, half))
        back = contract_last(tok[h, 1, n], held[h, 2])
        for term, lanes in ((both, slice(0, 2 * f)), (back, slice(2 * f, 3 * f))):
            term = term.reshape(NY, share, -1)
            if h:
                term = term + part32[n, :, :, lanes]
                part16[n, :, :, lanes] = term.astype(BF16)
            part32[n, :, :, lanes] = term
        if h:
            for d in (1, 3, 2):
                to = lax.rem(y + d, NY)
                send(part16.at[n, to], part_in.at[n, NY - d - 1], SUM, yr.at[n], at(dy=d))

    def stage_act(n):
        arrived(part_in.at[n], yr.at[n])
        total = part32[n, y] + (part_in[n, 0].astype(F32) + part_in[n, 1].astype(F32) + part_in[n, 2].astype(F32))
        gate, up, hidden_back = [total[:, i * f:(i + 1) * f] for i in range(3)]
        sigma = jax.nn.sigmoid(gate)
        gate_back = hidden_back * up * sigma * (1.0 + gate * (1.0 - sigma))
        up_back = hidden_back * gate * sigma
        hidden = gate * sigma * up
        act[n, y] = jnp.concatenate([gate_back, up_back, hidden], axis=1).astype(BF16)
        for d in (1, 3, 2):
            send(act.at[n, y], act.at[n, y], ACT, hr.at[n], at(dy=d))
        send(act.at[n, y], act_other.at[n, y], PASS, kr.at[n], neighbour)

    def stage_out(n):
        arrived(part_in.at[n], hr.at[n])
        for p in (1, 3, 2):
            place = lax.rem(y + p, NY)
            send(act.at[n, place], act_other.at[n, place], PASS, kr.at[n], neighbour)

        def outputs(ref, w, i):
            if i == 0:
                return matmul(ref[n, :, :, 2 * f:].reshape(rows, f), w[2])
            return matmul(ref[n, :, :, :2 * f].reshape(rows, 2 * f), w[0:2].reshape(2 * f, half))

        mine = [outputs(act, held.at[0], i) for i in range(2)]
        if n == 0:
            arrived(other, wr.at[0])
        arrived(act_other.at[n], kr.at[n])
        for i in range(2):
            value = (mine[i] + outputs(act_other, other, i)).reshape(NX, ROWS, half)
            own[n, i] = value[0]
            xsend[n, i] = value[1:].astype(BF16)
            for d in (1, 3, 2):
                send(xsend.at[n, i, d - 1], xin.at[n, i, NX - d - 1], OUT, ur.at[n, i], at(dx=d))

    step = ROWS // 4

    def stage_z(n):
        for i in range(2):
            arrived(xin.at[n, i], ur.at[n, i])
            value = own[n, i] + (xin[n, i, 0].astype(F32) + xin[n, i, 1].astype(F32) + xin[n, i, 2].astype(F32))
            for k in range(4):
                for j in range(4):
                    zf[n, i, k, j * step:(j + 1) * step] = value[k * step:(k + 1) * step, j * piece:(j + 1) * piece]
            zsend[n, i] = zf[n, i].astype(BF16)
            if n == 0:
                for m, (lo, k) in enumerate(group):
                    send(zsend.at[0, i, lo * 2 + k], zin.at[0, i, m + 1], NEAR, vr.at[0, i], at(lo=lo, k=k))
            else:
                for lo in range(2):
                    for k in range(2):
                        send(zsend.at[n, i, lo * 2 + k], zin.at[NQ - n, i, c], FAR, vr.at[NQ - n, i], at(dz=n, lo=lo, k=k))

    def last():
        for i, ref in enumerate((out_ref, back_ref)):
            arrived(zin.at[0, i, pl.ds(1, 3)], vr.at[0, i])
            same = zf[0, i, c] + zin[0, i, 1].astype(F32)
            cross = zin[0, i, 2].astype(F32) + zin[0, i, 3].astype(F32)
            sums = [jnp.where(core == 0, same, cross), jnp.where(core == 0, cross, same)]
            for q in ORDER[1:]:
                arrived(zin.at[q, i], vr.at[q, i])
                for k in range(2):
                    sums[k] = sums[k] + (zin[q, i, k].astype(F32) + zin[q, i, 2 + k].astype(F32))
            for k in range(2):
                for j in range(4):
                    ref[:, k * half + j * piece:k * half + (j + 1) * piece] = (
                        sums[k][j * step:(j + 1) * step].astype(BF16)
                    )

    def store_tokens():
        for h in range(2):
            for i in range(2):
                pltpu.make_async_copy(tok.at[h, i], tok_out.at[i, :, :, features(h)], store_sem.at[0]).start()

    def store_act(n):
        pltpu.make_async_copy(act.at[n], act_out.at[n], store_sem.at[1]).start()

    for lo in range(2):
        send(shard(0, 0), shard(slot, 0), Z, zr.at[slot], at(dz=shift, lo=lo))
    send(shard(0, 0), shard(2, 0), Z, zr.at[2], at(dz=2, lo=1 - z_lo))
    stage_x(0)
    stage_x(1)
    stage_x(3)
    stage_core(0)
    stage_mm(0, 0)
    stage_pass(1)
    stage_mm(0, 1)
    stage_x(2)
    stage_pass(3)
    stage_core(1)
    stage_weight(0)
    stage_mm(1, 0)
    stage_core(3)
    stage_weight(1)
    stage_mm(1, 1)
    stage_mm(3, 0)
    stage_act(0)
    stage_mm(3, 1)
    stage_core(2)
    stage_weight(2)
    stage_mm(2, 0)
    stage_mm(2, 1)
    store_tokens()
    stage_act(1)
    stage_act(3)
    stage_out(0)
    stage_act(2)
    stage_out(1)
    stage_out(3)
    stage_z(0)
    stage_out(2)
    for n in ORDER:
        store_act(n)
    stage_z(1)
    stage_z(3)
    stage_z(2)
    last()
    left(tok.at[0, :, 0, pl.ds(0, 3 * ROWS)], Z)
    left(tok.at[0, :, pl.ds(0, 3)], X)
    left(tok.at[0], CORE)
    left(other, WEIGHT)
    left(part_in, SUM)
    left(part_in, ACT)
    left(act, PASS)
    left(xin, OUT)
    left(zin.at[0, :, pl.ds(1, 3)], NEAR)
    left(zin.at[pl.ds(1, 3)], FAR)
    pltpu.make_async_copy(tok, tok, store_sem.at[0]).wait()
    pltpu.make_async_copy(act, act, store_sem.at[1]).wait()


def grads_kernel(out_ref, back_ref, tok_ref, act_ref, out_copy, back_copy, gate_grad, up_grad, down_grad):
    @pl.when(pl.program_id(0) == 0)
    def _():
        out_copy[...] = out_ref[...]
        back_copy[...] = back_ref[...]

    f = act_ref.shape[-1] // 3
    tokens, cot = [tok_ref[i].reshape(-1, tok_ref.shape[-1]) for i in range(2)]
    act = act_ref[...].reshape(-1, 3 * f)
    both = contract_first(act[:, :2 * f], tokens).astype(BF16)
    gate_grad[...] = both[:f]
    up_grad[...] = both[f:]
    down_grad[...] = contract_first(act[:, 2 * f:], cot).astype(BF16)


def weight_grads(out, back, tok, act):
    d, f = tok.shape[-1], act.shape[-1] // 3
    tile = 1024
    whole = pl.BlockSpec(out.shape, lambda i: (0, 0))
    grad = pl.BlockSpec((f, tile), lambda i: (0, i))
    small = jax.ShapeDtypeStruct(out.shape, BF16)
    large = jax.ShapeDtypeStruct((f, d), BF16)
    return pl.pallas_call(
        grads_kernel,
        grid=(d // tile,),
        out_shape=[small, small, large, large, large],
        in_specs=[
            whole, whole,
            pl.BlockSpec(tok.shape[:-1] + (tile,), lambda i: (0,) * (tok.ndim - 1) + (i,)),
            pl.BlockSpec(act.shape, lambda i: (0,) * act.ndim),
        ],
        out_specs=[whole, whole, grad, grad, grad],
        compiler_params=pltpu.CompilerParams(vmem_limit_bytes=56 * 2**20),
        name="grads",
    )(out, back, tok, act)


def on_device(tokens_in, cotangent, w_gate, w_up, w_down):
    d, f = w_gate.shape
    half = d // 2
    piece = half // 4
    group = NX * ROWS
    share = group // NY
    tokens = NQ * group
    dma = pltpu.SemaphoreType.DMA
    vmem = pl.BlockSpec(memory_space=pltpu.VMEM)
    hbm = pl.BlockSpec(memory_space=pltpu.HBM)
    out, back, tok, act = pl.pallas_call(
        block_kernel,
        out_shape=[
            jax.ShapeDtypeStruct((4, d), BF16),
            jax.ShapeDtypeStruct((4, d), BF16),
            jax.ShapeDtypeStruct((2, NQ, group, d), BF16),
            jax.ShapeDtypeStruct((NQ, NY, share, 3 * f), BF16),
        ],
        in_specs=[vmem, vmem, hbm, hbm, hbm],
        out_specs=[vmem, vmem, hbm, hbm],
        scratch_shapes=[
            pltpu.VMEM((2, 2, NQ, group, half), BF16),
            pltpu.VMEM((2, 3, f, half), BF16),
            pltpu.VMEM((3, f, half), BF16),
            pltpu.VMEM((NQ, NY, share, 3 * f), F32),
            pltpu.VMEM((NQ, NY, share, 3 * f), BF16),
            pltpu.VMEM((NQ, NY - 1, share, 3 * f), BF16),
            pltpu.VMEM((NQ, NY, share, 3 * f), BF16),
            pltpu.VMEM((NQ, NY, share, 3 * f), BF16),
            pltpu.VMEM((NQ, 2, ROWS, half), F32),
            pltpu.VMEM((NQ, 2, NX - 1, ROWS, half), BF16),
            pltpu.VMEM((NQ, 2, NX - 1, ROWS, half), BF16),
            pltpu.VMEM((NQ, 2, 4, ROWS, piece), F32),
            pltpu.VMEM((NQ, 2, 4, ROWS, piece), BF16),
            pltpu.VMEM((NQ, 2, 4, ROWS, piece), BF16),
            dma((2,)),
            dma((2,)),
            dma((10,)),
            dma((1,)),
            dma((NQ,)),
            dma((NQ, NX)),
            dma((NQ,)),
            dma((NQ,)),
            dma((NQ,)),
            dma((NQ,)),
            dma((NQ, 2)),
            dma((NQ, 2)),
        ],
        compiler_params=pltpu.CompilerParams(
            collective_id=0, has_side_effects=True, vmem_limit_bytes=56 * 2**20
        ),
        cost_estimate=pl.CostEstimate(flops=12 * tokens * d * f, bytes_accessed=6 * d * f, transcendentals=tokens * f),
        name="block",
    )(tokens_in, cotangent, w_gate.T, w_up.T, w_down)
    out, back, gate_grad, up_grad, down_grad = weight_grads(out, back, tok, act)
    return (out, back, gate_grad.T, up_grad.T, down_grad)


def solution(mesh):
    return jax.shard_map(
        on_device,
        mesh=mesh,
        in_specs=(
            P("rows", "depth"),
            P("rows", "depth"),
            P("depth", ("rows", "cols")),
            P("depth", ("rows", "cols")),
            P(("rows", "cols"), "depth"),
        ),
        out_specs=(
            P(("rows", "cols"), "depth"),
            P(("rows", "cols"), "depth"),
            P("depth", ("rows", "cols")),
            P("depth", ("rows", "cols")),
            P(("rows", "cols"), "depth"),
        ),
        check_vma=False,
    )
```

```python
import functools

import jax
import jax.numpy as jnp
from jax import lax
from jax.experimental import pallas as pl
from jax.experimental.pallas import tpu as pltpu
from jax.sharding import PartitionSpec as P

MESH = pl.DeviceIdType.MESH
F32 = jnp.float32
BF16 = jnp.bfloat16
NQ = 4
NX = 4
NY = 4
ORDER = [0, 1, 3, 2]
ROWS = 16


def contract_last(left, right):
    return lax.dot_general(
        left, right, (((1,), (1,)), ((), ())), preferred_element_type=F32
    )


def matmul(left, right):
    return jnp.dot(left, right, preferred_element_type=F32)


def contract_first(left, right):
    return lax.dot_general(
        left, right, (((0,), (0,)), ((), ())), preferred_element_type=F32
    )


def block_kernel(
    tokens_ref, cot_ref, w_gate_ref, w_up_ref, w_down_ref,
    out_ref, back_ref, tok_out, hidden_out, backs_out,
    tok, held, other, sum_a, sum_b, part_a, part_b, in_a, in_b, act_a, act_b, other_a, other_b,
    own, xsend, xin, zf, zsend, zin,
    load_sem, store_sem, sent, wr, zr, xr, cr, yr, hr, kr, ur, vr,
):
    r, c, y = lax.axis_index("rows"), lax.axis_index("cols"), lax.axis_index("depth")
    z_hi, x = r // NX, r % NX
    z_lo, core = c // 2, c % 2
    half = tok.shape[-1]
    f = held.shape[2]
    piece = half // 4
    weights = (w_gate_ref, w_up_ref, w_down_ref)
    sums, parts, parts_in = (sum_a, sum_b), (part_a, part_b), (in_a, in_b)
    acts, acts_other, acts_out = (act_a, act_b), (other_a, other_b), (hidden_out, backs_out)

    def at(dz=0, dx=0, lo=None, k=None, dy=0):
        lo = z_lo if lo is None else lo
        k = core if k is None else k
        row = lax.rem(z_hi + dz, NQ) * NX + lax.rem(x + dx, NX)
        return (row, lo * 2 + k, lax.rem(y + dy, NY))

    def features(h):
        return pl.ds(pl.multiple_of((core + h) % 2 * half, half), half)

    for a, ref in enumerate((tokens_ref, cot_ref)):
        pltpu.make_async_copy(ref.at[:, features(0)], tok.at[0, a, 0, pl.ds(0, ROWS)], load_sem.at[2]).start()

    barrier = pltpu.get_barrier_semaphore()
    neighbour = at(k=1 - core)
    group = [(1 - z_lo, core), (z_lo, 1 - core), (1 - z_lo, 1 - core)]
    partners = [at(dx=d) for d in range(1, NX)] + [at(dy=d) for d in range(1, NY)]
    partners += [at(dz=d, lo=lo, k=k) for d in range(1, NQ) for lo in range(2) for k in range(2)]
    partners += [at(lo=lo, k=k) for lo, k in group]
    for partner in partners:
        pl.semaphore_signal(barrier, inc=1, device_id=partner, device_id_type=MESH)

    for h in range(2):
        for i, ref in enumerate(weights):
            pltpu.make_async_copy(ref.at[:, features(h)], held.at[h, i], load_sem.at[h]).start()

    own_shard = tok.at[0, :, 0, pl.ds(0, ROWS)]
    pltpu.make_async_copy(own_shard, own_shard, load_sem.at[2]).wait()
    pl.semaphore_wait(barrier, len(partners))

    Z, X, CORE, WEIGHT, SUM_A, SUM_B, ACT_A, ACT_B, PASS_A, PASS_B, OUT, NEAR, FAR = range(13)

    def send(src, dst, kind, rs, to):
        pltpu.make_async_remote_copy(
            src_ref=src, dst_ref=dst, send_sem=sent.at[kind], recv_sem=rs, device_id=to, device_id_type=MESH
        ).start()

    def arrived(dst, rs):
        pltpu.make_async_remote_copy(
            src_ref=dst, dst_ref=dst, send_sem=sent.at[0], recv_sem=rs, device_id=neighbour, device_id_type=MESH
        ).wait_recv()

    def left(size, kind):
        pltpu.make_async_remote_copy(
            src_ref=size, dst_ref=size, send_sem=sent.at[kind], recv_sem=wr.at[0], device_id=neighbour, device_id_type=MESH
        ).wait_send()

    def shard(a, q, p):
        return tok.at[0, a, q, pl.ds(p * ROWS, ROWS)]

    up = 3 - 2 * z_lo
    steps = (0, up, 2, NQ - up)

    def stage_z_in(a):
        send(shard(a, 0, 0), shard(a, 1, 0), Z, zr.at[a, 1], at(dz=up, lo=1 - z_lo))
        send(shard(a, 0, 0), shard(a, 3, 0), Z, zr.at[a, 3], at(dz=up))
        send(shard(a, 0, 0), shard(a, 2, 0), Z, zr.at[a, 2], at(dz=2, lo=1 - z_lo))

    def stage_x(a, q):
        if q:
            arrived(shard(a, q, 0), zr.at[a, q])
        for d in (1, 3, 2):
            send(shard(a, q, 0), shard(a, q, NX - d), X, xr.at[a, q], at(dx=d))

    def stage_core(a, q):
        arrived(tok.at[0, a, q, pl.ds(ROWS, 3 * ROWS)], xr.at[a, q])
        send(tok.at[0, a, q], tok.at[1, a, q], CORE, cr.at[a, q], neighbour)

    def stage_weights():
        for i in (2, 0, 1):
            send(weights[i].at[:, features(1)], other.at[i], WEIGHT, wr.at[0], neighbour)

    rows = NX * ROWS
    share = rows // NY

    def stage_mm(a, n, h):
        if n == 0 and a == 0:
            pltpu.make_async_copy(held.at[h], held.at[h], load_sem.at[h]).wait()
        if h:
            arrived(tok.at[1, a, n], cr.at[a, n])
        w = held[h, 2] if a else held[h, 0:2].reshape(2 * f, half)
        term = contract_last(tok[h, a, n], w).reshape(NY, share, -1)
        if h:
            term = term + sums[a][n]
            parts[a][n] = term.astype(BF16)
        sums[a][n] = term
        if h:
            for d in (1, 3, 2):
                to = lax.rem(y + d, NY)
                send(parts[a].at[n, to], parts_in[a].at[n, NY - d - 1], SUM_A + a, yr.at[a, n], at(dy=d))

    def stage_act(a, n):
        arrived(parts_in[a].at[n], yr.at[a, n])
        into = parts_in[a]
        total = sums[a][n, y] + (into[n, 0].astype(F32) + into[n, 1].astype(F32) + into[n, 2].astype(F32))
        if a == 0:
            sum_a[n, y] = total
            gate, up_sum = total[:, :f], total[:, f:]
            act_a[n, y] = (gate * jax.nn.sigmoid(gate) * up_sum).astype(BF16)
        else:
            gate, up_sum = sum_a[n, y, :, :f], sum_a[n, y, :, f:]
            sigma = jax.nn.sigmoid(gate)
            gate_back = total * up_sum * sigma * (1.0 + gate * (1.0 - sigma))
            act_b[n, y] = jnp.concatenate([gate_back, total * gate * sigma], axis=1).astype(BF16)
        for d in (1, 3, 2):
            send(acts[a].at[n, y], acts[a].at[n, y], ACT_A + a, hr.at[a, n], at(dy=d))
        send(acts[a].at[n, y], acts_other[a].at[n, y], PASS_A + a, kr.at[a, n], neighbour)

    def stage_out(a, n):
        arrived(parts_in[1 - a].at[n], hr.at[a, n])
        for p in (1, 3, 2):
            place = lax.rem(y + p, NY)
            send(acts[a].at[n, place], acts_other[a].at[n, place], PASS_A + a, kr.at[a, n], neighbour)

        def output(ref, w):
            left_side = ref[n].reshape(rows, -1)
            return matmul(left_side, w[0:2].reshape(2 * f, half) if a else w[2])

        mine = output(acts[a], held.at[0])
        if n == 0 and a == 0:
            arrived(other, wr.at[0])
        arrived(acts_other[a].at[n], kr.at[a, n])
        value = (mine + output(acts_other[a], other)).reshape(NX, ROWS, half)
        own[n, a] = value[0]
        xsend[n, a] = value[1:].astype(BF16)
        for d in (1, 3, 2):
            send(xsend.at[n, a, d - 1], xin.at[n, a, NX - d - 1], OUT, ur.at[a, n], at(dx=d))

    step = ROWS // 4

    def stage_z(a, n):
        arrived(xin.at[n, a], ur.at[a, n])
        value = own[n, a] + (xin[n, a, 0].astype(F32) + xin[n, a, 1].astype(F32) + xin[n, a, 2].astype(F32))
        for k in range(4):
            for j in range(4):
                zf[n, a, k, j * step:(j + 1) * step] = value[k * step:(k + 1) * step, j * piece:(j + 1) * piece]
        zsend[n, a] = zf[n, a].astype(BF16)
        if n == 0:
            for m, (lo, k) in enumerate(group):
                send(zsend.at[0, a, lo * 2 + k], zin.at[0, a, m + 1], NEAR, vr.at[a, 0], at(lo=lo, k=k))
        else:
            for differs in range(2):
                lo = 1 - z_lo if differs else z_lo
                back = 2 if n == 2 else 1 if differs == (n == 1) else 3
                for k in range(2):
                    send(zsend.at[n, a, lo * 2 + k], zin.at[back, a, c], FAR, vr.at[a, back], at(dz=steps[n], lo=lo, k=k))

    def last(a, ref):
        arrived(zin.at[0, a, pl.ds(1, 3)], vr.at[a, 0])
        same = zf[0, a, c] + zin[0, a, 1].astype(F32)
        cross = zin[0, a, 2].astype(F32) + zin[0, a, 3].astype(F32)
        totals = [jnp.where(core == 0, same, cross), jnp.where(core == 0, cross, same)]
        for q in ORDER[1:]:
            arrived(zin.at[q, a], vr.at[a, q])
            for k in range(2):
                totals[k] = totals[k] + (zin[q, a, k].astype(F32) + zin[q, a, 2 + k].astype(F32))
        for k in range(2):
            for j in range(4):
                ref[:, k * half + j * piece:k * half + (j + 1) * piece] = (
                    totals[k][j * step:(j + 1) * step].astype(BF16)
                )

    def store_tokens():
        for h in range(2):
            for i in range(2):
                pltpu.make_async_copy(tok.at[h, i], tok_out.at[i, :, :, features(h)], store_sem.at[0]).start()

    def store_acts(a):
        pltpu.make_async_copy(acts[a], acts_out[a], store_sem.at[1 + a]).start()

    stage_z_in(0)
    stage_x(0, 0)
    stage_z_in(1)
    stage_x(1, 0)
    stage_x(0, 1)
    stage_core(0, 0)
    stage_mm(0, 0, 0)
    stage_x(0, 3)
    stage_mm(0, 0, 1)
    stage_core(1, 0)
    stage_x(0, 2)
    stage_x(1, 1)
    stage_mm(1, 0, 0)
    stage_mm(1, 0, 1)
    stage_x(1, 3)
    stage_core(0, 1)
    stage_mm(0, 1, 0)
    stage_x(1, 2)
    stage_core(0, 3)
    stage_mm(0, 1, 1)
    stage_mm(0, 3, 0)
    stage_act(0, 0)
    stage_mm(0, 3, 1)
    stage_core(0, 2)
    stage_core(1, 1)
    stage_weights()
    stage_act(1, 0)
    stage_mm(0, 2, 0)
    stage_mm(0, 2, 1)
    stage_mm(1, 1, 0)
    stage_mm(1, 1, 1)
    stage_core(1, 3)
    stage_act(0, 1)
    stage_mm(1, 3, 0)
    stage_mm(1, 3, 1)
    stage_core(1, 2)
    stage_act(0, 3)
    stage_mm(1, 2, 0)
    stage_mm(1, 2, 1)
    stage_out(0, 0)
    stage_act(1, 1)
    stage_act(0, 2)
    stage_out(1, 0)
    store_tokens()
    stage_act(1, 3)
    stage_out(0, 1)
    stage_act(1, 2)
    stage_out(0, 3)
    stage_out(1, 1)
    stage_out(0, 2)
    store_acts(0)
    stage_z(0, 0)
    stage_out(1, 3)
    stage_z(1, 0)
    stage_z(0, 1)
    stage_out(1, 2)
    store_acts(1)
    stage_z(0, 3)
    stage_z(1, 1)
    stage_z(0, 2)
    stage_z(1, 3)
    stage_z(1, 2)
    last(0, out_ref)
    last(1, back_ref)
    left(tok.at[0, :, 0, pl.ds(0, 3 * ROWS)], Z)
    left(tok.at[0, :, pl.ds(0, 3)], X)
    left(tok.at[0], CORE)
    left(other, WEIGHT)
    left(in_a, SUM_A)
    left(in_b, SUM_B)
    left(in_b, ACT_A)
    left(in_a, ACT_B)
    left(act_a, PASS_A)
    left(act_b, PASS_B)
    left(xin, OUT)
    left(zin.at[0, :, pl.ds(1, 3)], NEAR)
    left(zin.at[pl.ds(1, 3)], FAR)
    pltpu.make_async_copy(tok, tok, store_sem.at[0]).wait()
    pltpu.make_async_copy(act_a, act_a, store_sem.at[1]).wait()
    pltpu.make_async_copy(act_b, act_b, store_sem.at[2]).wait()


def grads_kernel(
    out_ref, back_ref, tok_ref, hidden_ref, backs_ref, out_copy, back_copy, gate_grad, up_grad, down_grad
):
    @pl.when(pl.program_id(0) == 0)
    def _():
        out_copy[...] = out_ref[...]
        back_copy[...] = back_ref[...]

    f = hidden_ref.shape[-1]
    tokens, cot = [tok_ref[i].reshape(-1, tok_ref.shape[-1]) for i in range(2)]
    both = contract_first(backs_ref[...].reshape(-1, 2 * f), tokens).astype(BF16)
    gate_grad[...] = both[:f]
    up_grad[...] = both[f:]
    down_grad[...] = contract_first(hidden_ref[...].reshape(-1, f), cot).astype(BF16)


def weight_grads(out, back, tok, hidden, backs):
    d, f = tok.shape[-1], hidden.shape[-1]
    tile = 1024
    whole = pl.BlockSpec(out.shape, lambda i: (0, 0))
    grad = pl.BlockSpec((f, tile), lambda i: (0, i))
    small = jax.ShapeDtypeStruct(out.shape, BF16)
    large = jax.ShapeDtypeStruct((f, d), BF16)
    return pl.pallas_call(
        grads_kernel,
        grid=(d // tile,),
        out_shape=[small, small, large, large, large],
        in_specs=[
            whole, whole,
            pl.BlockSpec(tok.shape[:-1] + (tile,), lambda i: (0,) * (tok.ndim - 1) + (i,)),
            pl.BlockSpec(hidden.shape, lambda i: (0,) * hidden.ndim),
            pl.BlockSpec(backs.shape, lambda i: (0,) * backs.ndim),
        ],
        out_specs=[whole, whole, grad, grad, grad],
        compiler_params=pltpu.CompilerParams(vmem_limit_bytes=56 * 2**20),
        name="grads",
    )(out, back, tok, hidden, backs)


def on_device(tokens_in, cotangent, w_gate, w_up, w_down):
    d, f = w_gate.shape
    half = d // 2
    piece = half // 4
    group = NX * ROWS
    share = group // NY
    tokens = NQ * group
    dma = pltpu.SemaphoreType.DMA
    vmem = pl.BlockSpec(memory_space=pltpu.VMEM)
    hbm = pl.BlockSpec(memory_space=pltpu.HBM)
    out, back, tok, hidden, backs = pl.pallas_call(
        block_kernel,
        out_shape=[
            jax.ShapeDtypeStruct((4, d), BF16),
            jax.ShapeDtypeStruct((4, d), BF16),
            jax.ShapeDtypeStruct((2, NQ, group, d), BF16),
            jax.ShapeDtypeStruct((NQ, NY, share, f), BF16),
            jax.ShapeDtypeStruct((NQ, NY, share, 2 * f), BF16),
        ],
        in_specs=[hbm] * 5,
        out_specs=[vmem, vmem, hbm, hbm, hbm],
        scratch_shapes=[
            pltpu.VMEM((2, 2, NQ, group, half), BF16),
            pltpu.VMEM((2, 3, f, half), BF16),
            pltpu.VMEM((3, f, half), BF16),
            pltpu.VMEM((NQ, NY, share, 2 * f), F32),
            pltpu.VMEM((NQ, NY, share, f), F32),
            pltpu.VMEM((NQ, NY, share, 2 * f), BF16),
            pltpu.VMEM((NQ, NY, share, f), BF16),
            pltpu.VMEM((NQ, NY - 1, share, 2 * f), BF16),
            pltpu.VMEM((NQ, NY - 1, share, f), BF16),
            pltpu.VMEM((NQ, NY, share, f), BF16),
            pltpu.VMEM((NQ, NY, share, 2 * f), BF16),
            pltpu.VMEM((NQ, NY, share, f), BF16),
            pltpu.VMEM((NQ, NY, share, 2 * f), BF16),
            pltpu.VMEM((NQ, 2, ROWS, half), F32),
            pltpu.VMEM((NQ, 2, NX - 1, ROWS, half), BF16),
            pltpu.VMEM((NQ, 2, NX - 1, ROWS, half), BF16),
            pltpu.VMEM((NQ, 2, 4, ROWS, piece), F32),
            pltpu.VMEM((NQ, 2, 4, ROWS, piece), BF16),
            pltpu.VMEM((NQ, 2, 4, ROWS, piece), BF16),
            dma((3,)),
            dma((3,)),
            dma((13,)),
            dma((1,)),
            dma((2, NQ)),
            dma((2, NQ)),
            dma((2, NQ)),
            dma((2, NQ)),
            dma((2, NQ)),
            dma((2, NQ)),
            dma((2, NQ)),
            dma((2, NQ)),
        ],
        compiler_params=pltpu.CompilerParams(
            collective_id=0, has_side_effects=True, vmem_limit_bytes=56 * 2**20
        ),
        cost_estimate=pl.CostEstimate(flops=12 * tokens * d * f, bytes_accessed=6 * d * f, transcendentals=tokens * f),
        name="block",
    )(tokens_in, cotangent, w_gate.T, w_up.T, w_down)
    out, back, gate_grad, up_grad, down_grad = weight_grads(out, back, tok, hidden, backs)
    return (out, back, gate_grad.T, up_grad.T, down_grad)


def solution(mesh):
    return jax.shard_map(
        on_device,
        mesh=mesh,
        in_specs=(
            P("rows", "depth"),
            P("rows", "depth"),
            P("depth", ("rows", "cols")),
            P("depth", ("rows", "cols")),
            P(("rows", "cols"), "depth"),
        ),
        out_specs=(
            P(("rows", "cols"), "depth"),
            P(("rows", "cols"), "depth"),
            P("depth", ("rows", "cols")),
            P("depth", ("rows", "cols")),
            P(("rows", "cols"), "depth"),
        ),
        check_vma=False,
    )
```

```python
import functools

import jax
import jax.numpy as jnp
from jax import lax
from jax.experimental import pallas as pl
from jax.experimental.pallas import tpu as pltpu
from jax.sharding import PartitionSpec as P

MESH = pl.DeviceIdType.MESH
F32 = jnp.float32
BF16 = jnp.bfloat16
NQ = 4
NX = 4
NY = 4
ORDER = [0, 1, 3, 2]
ROWS = 16


def contract_last(left, right):
    return lax.dot_general(
        left, right, (((1,), (1,)), ((), ())), preferred_element_type=F32
    )


def matmul(left, right):
    return jnp.dot(left, right, preferred_element_type=F32)


def contract_first(left, right):
    return lax.dot_general(
        left, right, (((0,), (0,)), ((), ())), preferred_element_type=F32
    )


def block_kernel(
    tokens_ref, cot_ref, w_gate_ref, w_up_ref, w_down_ref,
    out_ref, back_ref, tok_out, hidden_out, backs_out,
    tok, held, other, sum_a, sum_b, part_a, part_b, in_a, in_b, act_a, act_b, other_a, other_b,
    own, xsend, xin, zf, zsend, zin,
    load_sem, store_sem, sent, wr, zr, xr, cr, yr, hr, kr, ur, vr,
):
    r, c, y = lax.axis_index("rows"), lax.axis_index("cols"), lax.axis_index("depth")
    z_hi, x = r // NX, r % NX
    z_lo, core = c // 2, c % 2
    half = tok.shape[-1]
    f = held.shape[2]
    piece = half // 4
    weights = (w_gate_ref, w_up_ref, w_down_ref)
    sums, parts, parts_in = (sum_a, sum_b), (part_a, part_b), (in_a, in_b)
    acts, acts_other, acts_out = (act_a, act_b), (other_a, other_b), (hidden_out, backs_out)

    def at(dz=0, dx=0, lo=None, k=None, dy=0):
        lo = z_lo if lo is None else lo
        k = core if k is None else k
        row = lax.rem(z_hi + dz, NQ) * NX + lax.rem(x + dx, NX)
        return (row, lo * 2 + k, lax.rem(y + dy, NY))

    def features(h):
        return pl.ds(pl.multiple_of((core + h) % 2 * half, half), half)

    for a, ref in enumerate((tokens_ref, cot_ref)):
        pltpu.make_async_copy(ref.at[:, features(0)], tok.at[0, a, 0, pl.ds(0, ROWS)], load_sem.at[2]).start()

    barrier = pltpu.get_barrier_semaphore()
    neighbour = at(k=1 - core)
    group = [(1 - z_lo, core), (z_lo, 1 - core), (1 - z_lo, 1 - core)]
    partners = [at(dx=d) for d in range(1, NX)] + [at(dy=d) for d in range(1, NY)]
    partners += [at(dz=d, lo=lo, k=k) for d in range(1, NQ) for lo in range(2) for k in range(2)]
    partners += [at(lo=lo, k=k) for lo, k in group]
    for partner in partners:
        pl.semaphore_signal(barrier, inc=1, device_id=partner, device_id_type=MESH)

    for h in range(2):
        for i, ref in enumerate(weights):
            pltpu.make_async_copy(ref.at[:, features(h)], held.at[h, i], load_sem.at[h]).start()

    own_shard = tok.at[0, :, 0, pl.ds(0, ROWS)]
    pltpu.make_async_copy(own_shard, own_shard, load_sem.at[2]).wait()
    pl.semaphore_wait(barrier, len(partners))

    Z, X, CORE, WEIGHT, SUM_A, SUM_B, ACT_A, ACT_B, PASS_A, PASS_B, OUT, NEAR, FAR = range(13)

    def send(src, dst, kind, rs, to):
        pltpu.make_async_remote_copy(
            src_ref=src, dst_ref=dst, send_sem=sent.at[kind], recv_sem=rs, device_id=to, device_id_type=MESH
        ).start()

    def arrived(dst, rs):
        pltpu.make_async_remote_copy(
            src_ref=dst, dst_ref=dst, send_sem=sent.at[0], recv_sem=rs, device_id=neighbour, device_id_type=MESH
        ).wait_recv()

    def left(size, kind):
        pltpu.make_async_remote_copy(
            src_ref=size, dst_ref=size, send_sem=sent.at[kind], recv_sem=wr.at[0], device_id=neighbour, device_id_type=MESH
        ).wait_send()

    def shard(a, q, p):
        return tok.at[0, a, q, pl.ds(p * ROWS, ROWS)]

    up = 3 - 2 * z_lo
    steps = (0, up, 2, NQ - up)

    def stage_z_in(a):
        send(shard(a, 0, 0), shard(a, 1, 0), Z, zr.at[a, 1], at(dz=up, lo=1 - z_lo))
        send(shard(a, 0, 0), shard(a, 3, 0), Z, zr.at[a, 3], at(dz=up))
        send(shard(a, 0, 0), shard(a, 2, 0), Z, zr.at[a, 2], at(dz=2, lo=1 - z_lo))

    def stage_x(a, q):
        if q:
            arrived(shard(a, q, 0), zr.at[a, q])
        for d in (1, 3, 2):
            send(shard(a, q, 0), shard(a, q, NX - d), X, xr.at[a, q], at(dx=d))

    def stage_core(a, q):
        arrived(tok.at[0, a, q, pl.ds(ROWS, 3 * ROWS)], xr.at[a, q])
        send(tok.at[0, a, q], tok.at[1, a, q], CORE, cr.at[a, q], neighbour)

    def stage_weights():
        for i in (2, 0, 1):
            send(weights[i].at[:, features(1)], other.at[i], WEIGHT, wr.at[0], neighbour)

    rows = NX * ROWS
    share = rows // NY

    def stage_mm(a, n, h, first):
        if first:
            pltpu.make_async_copy(held.at[h], held.at[h], load_sem.at[h]).wait()
        if h:
            arrived(tok.at[1, a, n], cr.at[a, n])
        w = held[h, 2] if a else held[h, 0:2].reshape(2 * f, half)
        term = contract_last(tok[h, a, n], w).reshape(NY, share, -1)
        if h:
            term = term + sums[a][n]
            parts[a][n] = term.astype(BF16)
        sums[a][n] = term
        if h:
            for d in (1, 3, 2):
                to = lax.rem(y + d, NY)
                send(parts[a].at[n, to], parts_in[a].at[n, NY - d - 1], SUM_A + a, yr.at[a, n], at(dy=d))

    def stage_act(a, n):
        arrived(parts_in[a].at[n], yr.at[a, n])
        into = parts_in[a]
        total = sums[a][n, y] + (into[n, 0].astype(F32) + into[n, 1].astype(F32) + into[n, 2].astype(F32))
        if a == 0:
            sum_a[n, y] = total
            gate, up_sum = total[:, :f], total[:, f:]
            act_a[n, y] = (gate * jax.nn.sigmoid(gate) * up_sum).astype(BF16)
        else:
            gate, up_sum = sum_a[n, y, :, :f], sum_a[n, y, :, f:]
            sigma = jax.nn.sigmoid(gate)
            gate_back = total * up_sum * sigma * (1.0 + gate * (1.0 - sigma))
            act_b[n, y] = jnp.concatenate([gate_back, total * gate * sigma], axis=1).astype(BF16)
        for d in (1, 3, 2):
            send(acts[a].at[n, y], acts[a].at[n, y], ACT_A + a, hr.at[a, n], at(dy=d))

    def stage_pass(a, n):
        arrived(parts_in[1 - a].at[n], hr.at[a, n])
        send(acts[a].at[n], acts_other[a].at[n], PASS_A + a, kr.at[a, n], neighbour)

    def stage_out(a, n, first):
        def output(ref, w):
            left_side = ref[n].reshape(rows, -1)
            return matmul(left_side, w[0:2].reshape(2 * f, half) if a else w[2])

        if first:
            arrived(other, wr.at[0])
        arrived(acts_other[a].at[n], kr.at[a, n])
        value = (output(acts[a], held.at[0]) + output(acts_other[a], other)).reshape(NX, ROWS, half)
        own[n, a] = value[0]
        xsend[n, a] = value[1:].astype(BF16)
        for d in (1, 3, 2):
            send(xsend.at[n, a, d - 1], xin.at[n, a, NX - d - 1], OUT, ur.at[a, n], at(dx=d))

    step = ROWS // 4

    def stage_z(a, n):
        arrived(xin.at[n, a], ur.at[a, n])
        value = own[n, a] + (xin[n, a, 0].astype(F32) + xin[n, a, 1].astype(F32) + xin[n, a, 2].astype(F32))
        for k in range(4):
            for j in range(4):
                zf[n, a, k, j * step:(j + 1) * step] = value[k * step:(k + 1) * step, j * piece:(j + 1) * piece]
        zsend[n, a] = zf[n, a].astype(BF16)
        if n == 0:
            for m, (lo, k) in enumerate(group):
                send(zsend.at[0, a, lo * 2 + k], zin.at[0, a, m + 1], NEAR, vr.at[a, 0], at(lo=lo, k=k))
        else:
            for differs in range(2):
                lo = 1 - z_lo if differs else z_lo
                back = 2 if n == 2 else 1 if differs == (n == 1) else 3
                for k in range(2):
                    send(zsend.at[n, a, lo * 2 + k], zin.at[back, a, c], FAR, vr.at[a, back], at(dz=steps[n], lo=lo, k=k))

    def last(a, ref):
        arrived(zin.at[0, a, pl.ds(1, 3)], vr.at[a, 0])
        same = zf[0, a, c] + zin[0, a, 1].astype(F32)
        cross = zin[0, a, 2].astype(F32) + zin[0, a, 3].astype(F32)
        totals = [jnp.where(core == 0, same, cross), jnp.where(core == 0, cross, same)]
        for q in ORDER[1:]:
            arrived(zin.at[q, a], vr.at[a, q])
            for k in range(2):
                totals[k] = totals[k] + (zin[q, a, k].astype(F32) + zin[q, a, 2 + k].astype(F32))
        for k in range(2):
            for j in range(4):
                ref[:, k * half + j * piece:k * half + (j + 1) * piece] = (
                    totals[k][j * step:(j + 1) * step].astype(BF16)
                )

    def store_tokens():
        for h in range(2):
            for i in range(2):
                pltpu.make_async_copy(tok.at[h, i], tok_out.at[i, :, :, features(h)], store_sem.at[0]).start()

    def store_acts(a):
        pltpu.make_async_copy(acts[a], acts_out[a], store_sem.at[1 + a]).start()

    stage_z_in(0)
    stage_x(0, 0)
    stage_weights()
    stage_x(1, 0)
    stage_z_in(1)
    stage_x(0, 1)
    stage_x(0, 3)
    stage_core(0, 0)
    stage_core(1, 0)
    stage_x(0, 2)
    stage_mm(0, 0, 0, True)
    stage_mm(0, 0, 1, True)
    stage_x(1, 3)
    stage_core(0, 1)
    stage_mm(1, 0, 0, False)
    stage_mm(0, 1, 0, False)
    stage_mm(1, 0, 1, False)
    stage_x(1, 2)
    stage_core(0, 3)
    stage_mm(0, 1, 1, False)
    stage_x(1, 1)
    stage_mm(0, 3, 0, False)
    stage_core(0, 2)
    stage_mm(0, 3, 1, False)
    stage_mm(0, 2, 0, False)
    stage_core(1, 3)
    stage_mm(0, 2, 1, False)
    stage_mm(1, 3, 0, False)
    stage_core(1, 2)
    stage_act(0, 0)
    stage_mm(1, 2, 0, False)
    stage_act(0, 1)
    stage_mm(1, 2, 1, False)
    stage_core(1, 1)
    stage_mm(1, 1, 0, False)
    stage_mm(1, 3, 1, False)
    stage_act(0, 3)
    stage_act(0, 2)
    stage_mm(1, 1, 1, False)
    store_tokens()
    stage_pass(0, 0)
    stage_pass(0, 1)
    stage_act(1, 2)
    stage_out(0, 0, True)
    stage_act(1, 3)
    stage_out(0, 1, False)
    stage_pass(0, 2)
    stage_pass(0, 3)
    stage_act(1, 1)
    stage_act(1, 0)
    stage_out(0, 2, False)
    stage_pass(1, 2)
    stage_out(0, 3, False)
    stage_pass(1, 3)
    stage_z(0, 0)
    stage_out(1, 2, False)
    stage_pass(1, 1)
    stage_out(1, 3, False)
    stage_pass(1, 0)
    stage_out(1, 1, False)
    stage_z(0, 2)
    stage_out(1, 0, False)
    store_acts(0)
    store_acts(1)
    stage_z(0, 1)
    stage_z(1, 2)
    stage_z(0, 3)
    stage_z(1, 3)
    stage_z(1, 1)
    stage_z(1, 0)
    last(0, out_ref)
    last(1, back_ref)
    left(tok.at[0, :, 0, pl.ds(0, 3 * ROWS)], Z)
    left(tok.at[0, :, pl.ds(0, 3)], X)
    left(tok.at[0], CORE)
    left(other, WEIGHT)
    left(in_a, SUM_A)
    left(in_b, SUM_B)
    left(in_b, ACT_A)
    left(in_a, ACT_B)
    left(act_a, PASS_A)
    left(act_b, PASS_B)
    left(xin, OUT)
    left(zin.at[0, :, pl.ds(1, 3)], NEAR)
    left(zin.at[pl.ds(1, 3)], FAR)
    pltpu.make_async_copy(tok, tok, store_sem.at[0]).wait()
    pltpu.make_async_copy(act_a, act_a, store_sem.at[1]).wait()
    pltpu.make_async_copy(act_b, act_b, store_sem.at[2]).wait()


def grads_kernel(
    out_ref, back_ref, tok_ref, hidden_ref, backs_ref, out_copy, back_copy, gate_grad, up_grad, down_grad
):
    @pl.when(pl.program_id(0) == 0)
    def _():
        out_copy[...] = out_ref[...]
        back_copy[...] = back_ref[...]

    f = hidden_ref.shape[-1]
    tokens, cot = [tok_ref[i].reshape(-1, tok_ref.shape[-1]) for i in range(2)]
    both = contract_first(backs_ref[...].reshape(-1, 2 * f), tokens).astype(BF16)
    gate_grad[...] = both[:f]
    up_grad[...] = both[f:]
    down_grad[...] = contract_first(hidden_ref[...].reshape(-1, f), cot).astype(BF16)


def weight_grads(out, back, tok, hidden, backs):
    d, f = tok.shape[-1], hidden.shape[-1]
    tile = 1024
    whole = pl.BlockSpec(out.shape, lambda i: (0, 0))
    grad = pl.BlockSpec((f, tile), lambda i: (0, i))
    small = jax.ShapeDtypeStruct(out.shape, BF16)
    large = jax.ShapeDtypeStruct((f, d), BF16)
    return pl.pallas_call(
        grads_kernel,
        grid=(d // tile,),
        out_shape=[small, small, large, large, large],
        in_specs=[
            whole, whole,
            pl.BlockSpec(tok.shape[:-1] + (tile,), lambda i: (0,) * (tok.ndim - 1) + (i,)),
            pl.BlockSpec(hidden.shape, lambda i: (0,) * hidden.ndim),
            pl.BlockSpec(backs.shape, lambda i: (0,) * backs.ndim),
        ],
        out_specs=[whole, whole, grad, grad, grad],
        compiler_params=pltpu.CompilerParams(vmem_limit_bytes=56 * 2**20),
        name="grads",
    )(out, back, tok, hidden, backs)


def on_device(tokens_in, cotangent, w_gate, w_up, w_down):
    d, f = w_gate.shape
    half = d // 2
    piece = half // 4
    group = NX * ROWS
    share = group // NY
    tokens = NQ * group
    dma = pltpu.SemaphoreType.DMA
    vmem = pl.BlockSpec(memory_space=pltpu.VMEM)
    hbm = pl.BlockSpec(memory_space=pltpu.HBM)
    out, back, tok, hidden, backs = pl.pallas_call(
        block_kernel,
        out_shape=[
            jax.ShapeDtypeStruct((4, d), BF16),
            jax.ShapeDtypeStruct((4, d), BF16),
            jax.ShapeDtypeStruct((2, NQ, group, d), BF16),
            jax.ShapeDtypeStruct((NQ, NY, share, f), BF16),
            jax.ShapeDtypeStruct((NQ, NY, share, 2 * f), BF16),
        ],
        in_specs=[hbm] * 5,
        out_specs=[vmem, vmem, hbm, hbm, hbm],
        scratch_shapes=[
            pltpu.VMEM((2, 2, NQ, group, half), BF16),
            pltpu.VMEM((2, 3, f, half), BF16),
            pltpu.VMEM((3, f, half), BF16),
            pltpu.VMEM((NQ, NY, share, 2 * f), F32),
            pltpu.VMEM((NQ, NY, share, f), F32),
            pltpu.VMEM((NQ, NY, share, 2 * f), BF16),
            pltpu.VMEM((NQ, NY, share, f), BF16),
            pltpu.VMEM((NQ, NY - 1, share, 2 * f), BF16),
            pltpu.VMEM((NQ, NY - 1, share, f), BF16),
            pltpu.VMEM((NQ, NY, share, f), BF16),
            pltpu.VMEM((NQ, NY, share, 2 * f), BF16),
            pltpu.VMEM((NQ, NY, share, f), BF16),
            pltpu.VMEM((NQ, NY, share, 2 * f), BF16),
            pltpu.VMEM((NQ, 2, ROWS, half), F32),
            pltpu.VMEM((NQ, 2, NX - 1, ROWS, half), BF16),
            pltpu.VMEM((NQ, 2, NX - 1, ROWS, half), BF16),
            pltpu.VMEM((NQ, 2, 4, ROWS, piece), F32),
            pltpu.VMEM((NQ, 2, 4, ROWS, piece), BF16),
            pltpu.VMEM((NQ, 2, 4, ROWS, piece), BF16),
            dma((3,)),
            dma((3,)),
            dma((13,)),
            dma((1,)),
            dma((2, NQ)),
            dma((2, NQ)),
            dma((2, NQ)),
            dma((2, NQ)),
            dma((2, NQ)),
            dma((2, NQ)),
            dma((2, NQ)),
            dma((2, NQ)),
        ],
        compiler_params=pltpu.CompilerParams(
            collective_id=0, has_side_effects=True, vmem_limit_bytes=56 * 2**20
        ),
        cost_estimate=pl.CostEstimate(flops=12 * tokens * d * f, bytes_accessed=6 * d * f, transcendentals=tokens * f),
        name="block",
    )(tokens_in, cotangent, w_gate.T, w_up.T, w_down)
    out, back, gate_grad, up_grad, down_grad = weight_grads(out, back, tok, hidden, backs)
    return (out, back, gate_grad.T, up_grad.T, down_grad)


def solution(mesh):
    return jax.shard_map(
        on_device,
        mesh=mesh,
        in_specs=(
            P("rows", "depth"),
            P("rows", "depth"),
            P("depth", ("rows", "cols")),
            P("depth", ("rows", "cols")),
            P(("rows", "cols"), "depth"),
        ),
        out_specs=(
            P(("rows", "cols"), "depth"),
            P(("rows", "cols"), "depth"),
            P("depth", ("rows", "cols")),
            P("depth", ("rows", "cols")),
            P(("rows", "cols"), "depth"),
        ),
        check_vma=False,
    )
```

```python
import functools

import jax
import jax.numpy as jnp
from jax import lax
from jax.experimental import pallas as pl
from jax.experimental.pallas import tpu as pltpu
from jax.sharding import PartitionSpec as P

MESH = pl.DeviceIdType.MESH
F32 = jnp.float32
BF16 = jnp.bfloat16
NQ = 4
NX = 4
NY = 4
ORDER = [0, 1, 3, 2]
ROWS = 16


def contract_last(left, right):
    return lax.dot_general(
        left, right, (((1,), (1,)), ((), ())), preferred_element_type=F32
    )


def matmul(left, right):
    return jnp.dot(left, right, preferred_element_type=F32)


def contract_first(left, right):
    return lax.dot_general(
        left, right, (((0,), (0,)), ((), ())), preferred_element_type=F32
    )


def block_kernel(
    tokens_ref, cot_ref, w_gate_ref, w_up_ref, w_down_ref,
    out_ref, back_ref, gate_grad, up_grad, down_grad,
    tok, held, other, sum_a, sum_b, part_a, part_b, in_a, in_b, act_a, act_b, other_a, other_b,
    own, xsend, xin, zf, zsend, zin,
    load_sem, sent, wr, zr, xr, cr, yr, hr, kr, ur, vr,
):
    r, c, y = lax.axis_index("rows"), lax.axis_index("cols"), lax.axis_index("depth")
    z_hi, x = r // NX, r % NX
    z_lo, core = c // 2, c % 2
    half = tok.shape[-1]
    f = held.shape[2]
    piece = half // 4
    weights = (w_gate_ref, w_up_ref, w_down_ref)
    sums, parts, parts_in = (sum_a, sum_b), (part_a, part_b), (in_a, in_b)
    acts, acts_other = (act_a, act_b), (other_a, other_b)

    def at(dz=0, dx=0, lo=None, k=None, dy=0):
        lo = z_lo if lo is None else lo
        k = core if k is None else k
        row = lax.rem(z_hi + dz, NQ) * NX + lax.rem(x + dx, NX)
        return (row, lo * 2 + k, lax.rem(y + dy, NY))

    def features(h):
        return pl.ds(pl.multiple_of((core + h) % 2 * half, half), half)

    for a, ref in enumerate((tokens_ref, cot_ref)):
        pltpu.make_async_copy(ref.at[:, features(0)], tok.at[0, a, 0, pl.ds(0, ROWS)], load_sem.at[2]).start()

    barrier = pltpu.get_barrier_semaphore()
    neighbour = at(k=1 - core)
    group = [(1 - z_lo, core), (z_lo, 1 - core), (1 - z_lo, 1 - core)]
    partners = [at(dx=d) for d in range(1, NX)] + [at(dy=d) for d in range(1, NY)]
    partners += [at(dz=d, lo=lo, k=k) for d in range(1, NQ) for lo in range(2) for k in range(2)]
    partners += [at(lo=lo, k=k) for lo, k in group]
    for partner in partners:
        pl.semaphore_signal(barrier, inc=1, device_id=partner, device_id_type=MESH)

    for h in range(2):
        for i, ref in enumerate(weights):
            pltpu.make_async_copy(ref.at[:, features(h)], held.at[h, i], load_sem.at[h]).start()

    own_shard = tok.at[0, :, 0, pl.ds(0, ROWS)]
    pltpu.make_async_copy(own_shard, own_shard, load_sem.at[2]).wait()
    pl.semaphore_wait(barrier, len(partners))

    Z, X, CORE, WEIGHT, SUM_A, SUM_B, ACT_A, ACT_B, PASS_A, PASS_B, OUT, NEAR, FAR = range(13)

    def send(src, dst, kind, rs, to):
        pltpu.make_async_remote_copy(
            src_ref=src, dst_ref=dst, send_sem=sent.at[kind], recv_sem=rs, device_id=to, device_id_type=MESH
        ).start()

    def arrived(dst, rs):
        pltpu.make_async_remote_copy(
            src_ref=dst, dst_ref=dst, send_sem=sent.at[0], recv_sem=rs, device_id=neighbour, device_id_type=MESH
        ).wait_recv()

    def left(size, kind):
        pltpu.make_async_remote_copy(
            src_ref=size, dst_ref=size, send_sem=sent.at[kind], recv_sem=wr.at[0], device_id=neighbour, device_id_type=MESH
        ).wait_send()

    def shard(a, q, p):
        return tok.at[0, a, q, pl.ds(p * ROWS, ROWS)]

    up = 3 - 2 * z_lo
    steps = (0, up, 2, NQ - up)

    def stage_z_in(a):
        send(shard(a, 0, 0), shard(a, 1, 0), Z, zr.at[a, 1], at(dz=up, lo=1 - z_lo))
        send(shard(a, 0, 0), shard(a, 3, 0), Z, zr.at[a, 3], at(dz=up))
        send(shard(a, 0, 0), shard(a, 2, 0), Z, zr.at[a, 2], at(dz=2, lo=1 - z_lo))

    def stage_x(a, q):
        if q:
            arrived(shard(a, q, 0), zr.at[a, q])
        for d in (1, 3, 2):
            send(shard(a, q, 0), shard(a, q, NX - d), X, xr.at[a, q], at(dx=d))

    def stage_core(a, q):
        arrived(tok.at[0, a, q, pl.ds(ROWS, 3 * ROWS)], xr.at[a, q])
        send(tok.at[0, a, q], tok.at[1, a, q], CORE, cr.at[a, q], neighbour)

    def stage_weights():
        for i in (2, 0, 1):
            send(weights[i].at[:, features(1)], other.at[i], WEIGHT, wr.at[0], neighbour)

    rows = NX * ROWS
    share = rows // NY

    def stage_mm(a, n, h, first):
        if first:
            pltpu.make_async_copy(held.at[h], held.at[h], load_sem.at[h]).wait()
        if h:
            arrived(tok.at[1, a, n], cr.at[a, n])
        w = held[h, 2] if a else held[h, 0:2].reshape(2 * f, half)
        term = contract_last(tok[h, a, n], w).reshape(NY, share, -1)
        if h:
            term = term + sums[a][n]
            parts[a][n] = term.astype(BF16)
        sums[a][n] = term
        if h:
            for d in (1, 3, 2):
                to = lax.rem(y + d, NY)
                send(parts[a].at[n, to], parts_in[a].at[n, NY - d - 1], SUM_A + a, yr.at[a, n], at(dy=d))

    def stage_act(a, n):
        arrived(parts_in[a].at[n], yr.at[a, n])
        into = parts_in[a]
        total = sums[a][n, y] + (into[n, 0].astype(F32) + into[n, 1].astype(F32) + into[n, 2].astype(F32))
        if a == 0:
            sum_a[n, y] = total
            gate, up_sum = total[:, :f], total[:, f:]
            act_a[n, y] = (gate * jax.nn.sigmoid(gate) * up_sum).astype(BF16)
        else:
            gate, up_sum = sum_a[n, y, :, :f], sum_a[n, y, :, f:]
            sigma = jax.nn.sigmoid(gate)
            gate_back = total * up_sum * sigma * (1.0 + gate * (1.0 - sigma))
            act_b[n, y] = jnp.concatenate([gate_back, total * gate * sigma], axis=1).astype(BF16)
        for d in (1, 3, 2):
            send(acts[a].at[n, y], acts[a].at[n, y], ACT_A + a, hr.at[a, n], at(dy=d))

    def stage_pass(a, n):
        arrived(parts_in[1 - a].at[n], hr.at[a, n])
        send(acts[a].at[n], acts_other[a].at[n], PASS_A + a, kr.at[a, n], neighbour)

    def stage_out(a, n, first):
        def output(ref, w):
            left_side = ref[n].reshape(rows, -1)
            return matmul(left_side, w[0:2].reshape(2 * f, half) if a else w[2])

        if first:
            arrived(other, wr.at[0])
        arrived(acts_other[a].at[n], kr.at[a, n])
        value = (output(acts[a], held.at[0]) + output(acts_other[a], other)).reshape(NX, ROWS, half)
        own[n, a] = value[0]
        xsend[n, a] = value[1:].astype(BF16)
        for d in (1, 3, 2):
            send(xsend.at[n, a, d - 1], xin.at[n, a, NX - d - 1], OUT, ur.at[a, n], at(dx=d))

    step = ROWS // 4

    def stage_z(a, n):
        arrived(xin.at[n, a], ur.at[a, n])
        value = own[n, a] + (xin[n, a, 0].astype(F32) + xin[n, a, 1].astype(F32) + xin[n, a, 2].astype(F32))
        for k in range(4):
            for j in range(4):
                zf[n, a, k, j * step:(j + 1) * step] = value[k * step:(k + 1) * step, j * piece:(j + 1) * piece]
        zsend[n, a] = zf[n, a].astype(BF16)
        if n == 0:
            for m, (lo, k) in enumerate(group):
                send(zsend.at[0, a, lo * 2 + k], zin.at[0, a, m + 1], NEAR, vr.at[a, 0], at(lo=lo, k=k))
        else:
            for differs in range(2):
                lo = 1 - z_lo if differs else z_lo
                back = 2 if n == 2 else 1 if differs == (n == 1) else 3
                for k in range(2):
                    send(zsend.at[n, a, lo * 2 + k], zin.at[back, a, c], FAR, vr.at[a, back], at(dz=steps[n], lo=lo, k=k))

    def last(a, ref):
        arrived(zin.at[0, a, pl.ds(1, 3)], vr.at[a, 0])
        same = zf[0, a, c] + zin[0, a, 1].astype(F32)
        cross = zin[0, a, 2].astype(F32) + zin[0, a, 3].astype(F32)
        totals = [jnp.where(core == 0, same, cross), jnp.where(core == 0, cross, same)]
        for q in ORDER[1:]:
            arrived(zin.at[q, a], vr.at[a, q])
            for k in range(2):
                totals[k] = totals[k] + (zin[q, a, k].astype(F32) + zin[q, a, 2 + k].astype(F32))
        for k in range(2):
            for j in range(4):
                ref[:, k * half + j * piece:k * half + (j + 1) * piece] = (
                    totals[k][j * step:(j + 1) * step].astype(BF16)
                )

    def stage_grad(i, h):
        held_act = act_a[...] if i == 2 else act_b[:, :, :, i * f:(i + 1) * f]
        left_side = held_act.reshape(NQ * rows, f)
        for j in range(2):
            right_side = tok[h, i // 2, :, :, j * half // 2:(j + 1) * half // 2].reshape(NQ * rows, half // 2)
            place = pl.multiple_of((core + h) % 2 * half + j * half // 2, half // 2)
            (gate_grad, up_grad, down_grad)[i][:, pl.ds(place, half // 2)] = contract_first(left_side, right_side).astype(BF16)

    stage_z_in(0)
    stage_x(0, 0)
    stage_weights()
    stage_x(1, 0)
    stage_z_in(1)
    stage_x(0, 1)
    stage_x(0, 3)
    stage_core(0, 0)
    stage_mm(0, 0, 0, True)
    stage_x(1, 1)
    stage_x(0, 2)
    stage_core(1, 0)
    stage_mm(0, 0, 1, True)
    stage_x(1, 3)
    stage_mm(1, 0, 0, False)
    stage_core(0, 1)
    stage_mm(1, 0, 1, False)
    stage_core(0, 3)
    stage_mm(0, 3, 0, False)
    stage_mm(0, 1, 0, False)
    stage_x(1, 2)
    stage_mm(0, 1, 1, False)
    stage_act(0, 0)
    stage_core(0, 2)
    stage_act(1, 0)
    stage_core(1, 1)
    stage_mm(0, 2, 0, False)
    stage_mm(1, 1, 0, False)
    stage_mm(0, 2, 1, False)
    stage_core(1, 3)
    stage_mm(0, 3, 1, False)
    stage_core(1, 2)
    stage_mm(1, 2, 0, False)
    stage_mm(1, 3, 0, False)
    stage_pass(0, 0)
    stage_mm(1, 2, 1, False)
    stage_act(0, 1)
    stage_mm(1, 1, 1, False)
    stage_pass(1, 0)
    stage_act(0, 2)
    stage_mm(1, 3, 1, False)
    stage_out(0, 0, True)
    stage_act(0, 3)
    stage_act(1, 2)
    stage_pass(0, 1)
    stage_out(1, 0, False)
    stage_act(1, 1)
    stage_pass(0, 2)
    stage_out(0, 1, False)
    stage_act(1, 3)
    stage_pass(0, 3)
    stage_out(0, 2, False)
    stage_grad(2, 0)
    stage_pass(1, 2)
    stage_out(0, 3, False)
    stage_z(0, 0)
    stage_pass(1, 1)
    stage_out(1, 2, False)
    stage_pass(1, 3)
    stage_out(1, 1, False)
    stage_out(1, 3, False)
    stage_z(0, 1)
    stage_z(0, 2)
    stage_grad(0, 1)
    stage_z(0, 3)
    stage_z(1, 2)
    stage_z(1, 1)
    stage_grad(2, 1)
    stage_z(1, 3)
    stage_z(1, 0)
    stage_grad(1, 1)
    stage_grad(1, 0)
    last(0, out_ref)
    stage_grad(0, 0)
    last(1, back_ref)
    left(tok.at[0, :, 0, pl.ds(0, 3 * ROWS)], Z)
    left(tok.at[0, :, pl.ds(0, 3)], X)
    left(tok.at[0], CORE)
    left(other, WEIGHT)
    left(in_a, SUM_A)
    left(in_b, SUM_B)
    left(in_b, ACT_A)
    left(in_a, ACT_B)
    left(act_a, PASS_A)
    left(act_b, PASS_B)
    left(xin, OUT)
    left(zin.at[0, :, pl.ds(1, 3)], NEAR)
    left(zin.at[pl.ds(1, 3)], FAR)


def write_kernel(*refs):
    n = len(refs) // 2
    copies = [pltpu.make_async_copy(refs[i], refs[n + i], refs[-1].at[i]) for i in range(n)]
    for copy in copies:
        copy.start()
    for copy in copies:
        copy.wait()


def write_out(arrays):
    n = len(arrays)
    return pl.pallas_call(
        write_kernel,
        out_shape=[jax.ShapeDtypeStruct(v.shape, v.dtype) for v in arrays],
        in_specs=[pl.BlockSpec(memory_space=pl.ANY)] * n,
        out_specs=[pl.BlockSpec(memory_space=pl.ANY)] * n,
        scratch_shapes=[pltpu.SemaphoreType.DMA((n,))],
        compiler_params=pltpu.CompilerParams(vmem_limit_bytes=2**20),
        name="write",
    )(*arrays)


def on_device(tokens_in, cotangent, w_gate, w_up, w_down):
    d, f = w_gate.shape
    half = d // 2
    piece = half // 4
    group = NX * ROWS
    share = group // NY
    tokens = NQ * group
    dma = pltpu.SemaphoreType.DMA
    vmem = pl.BlockSpec(memory_space=pltpu.VMEM)
    hbm = pl.BlockSpec(memory_space=pltpu.HBM)
    results = pl.pallas_call(
        block_kernel,
        out_shape=[
            jax.ShapeDtypeStruct((4, d), BF16),
            jax.ShapeDtypeStruct((4, d), BF16),
            jax.ShapeDtypeStruct((f, d), BF16),
            jax.ShapeDtypeStruct((f, d), BF16),
            jax.ShapeDtypeStruct((f, d), BF16),
        ],
        in_specs=[hbm] * 5,
        out_specs=[vmem] * 5,
        scratch_shapes=[
            pltpu.VMEM((2, 2, NQ, group, half), BF16),
            pltpu.VMEM((2, 3, f, half), BF16),
            pltpu.VMEM((3, f, half), BF16),
            pltpu.VMEM((NQ, NY, share, 2 * f), F32),
            pltpu.VMEM((NQ, NY, share, f), F32),
            pltpu.VMEM((NQ, NY, share, 2 * f), BF16),
            pltpu.VMEM((NQ, NY, share, f), BF16),
            pltpu.VMEM((NQ, NY - 1, share, 2 * f), BF16),
            pltpu.VMEM((NQ, NY - 1, share, f), BF16),
            pltpu.VMEM((NQ, NY, share, f), BF16),
            pltpu.VMEM((NQ, NY, share, 2 * f), BF16),
            pltpu.VMEM((NQ, NY, share, f), BF16),
            pltpu.VMEM((NQ, NY, share, 2 * f), BF16),
            pltpu.VMEM((NQ, 2, ROWS, half), F32),
            pltpu.VMEM((NQ, 2, NX - 1, ROWS, half), BF16),
            pltpu.VMEM((NQ, 2, NX - 1, ROWS, half), BF16),
            pltpu.VMEM((NQ, 2, 4, ROWS, piece), F32),
            pltpu.VMEM((NQ, 2, 4, ROWS, piece), BF16),
            pltpu.VMEM((NQ, 2, 4, ROWS, piece), BF16),
            dma((3,)),
            dma((13,)),
            dma((1,)),
            dma((2, NQ)),
            dma((2, NQ)),
            dma((2, NQ)),
            dma((2, NQ)),
            dma((2, NQ)),
            dma((2, NQ)),
            dma((2, NQ)),
            dma((2, NQ)),
        ],
        compiler_params=pltpu.CompilerParams(
            collective_id=0, has_side_effects=True, vmem_limit_bytes=40 * 2**20
        ),
        cost_estimate=pl.CostEstimate(flops=12 * tokens * d * f, bytes_accessed=6 * d * f, transcendentals=tokens * f),
        name="block",
    )(*[
        pltpu.with_memory_space_constraint(v, pltpu.HBM)
        for v in (tokens_in, cotangent, w_gate.T, w_up.T, w_down)
    ])
    out, back, gate_grad, up_grad, down_grad = write_out(results)
    return (out, back, gate_grad.T, up_grad.T, down_grad)


def solution(mesh):
    return jax.shard_map(
        on_device,
        mesh=mesh,
        in_specs=(
            P("rows", "depth"),
            P("rows", "depth"),
            P("depth", ("rows", "cols")),
            P("depth", ("rows", "cols")),
            P(("rows", "cols"), "depth"),
        ),
        out_specs=(
            P(("rows", "cols"), "depth"),
            P(("rows", "cols"), "depth"),
            P("depth", ("rows", "cols")),
            P("depth", ("rows", "cols")),
            P(("rows", "cols"), "depth"),
        ),
        check_vma=False,
    )
```

```python
import functools

import jax
import jax.numpy as jnp
from jax import lax
from jax.experimental import pallas as pl
from jax.experimental.pallas import tpu as pltpu
from jax.sharding import PartitionSpec as P

MESH = pl.DeviceIdType.MESH
F32 = jnp.float32
BF16 = jnp.bfloat16
NQ = 4
NX = 4
NY = 4
ORDER = [0, 1, 3, 2]
ROWS = 16


def contract_last(left, right):
    return lax.dot_general(
        left, right, (((1,), (1,)), ((), ())), preferred_element_type=F32
    )


def matmul(left, right):
    return jnp.dot(left, right, preferred_element_type=F32)


def contract_first(left, right):
    return lax.dot_general(
        left, right, (((0,), (0,)), ((), ())), preferred_element_type=F32
    )


def block_kernel(
    tokens_ref, cot_ref, w_gate_ref, w_up_ref, w_down_ref,
    out_ref, back_ref, gate_grad, up_grad, down_grad,
    tok, held, other, sum_a, sum_b, part_a, part_b, in_a, in_b, act_a, act_b, other_a, other_b,
    own, xsend, xin, zf, zsend, zin,
    load_sem, sent, wr, zr, xr, cr, yr, hr, kr, ur, vr,
):
    r, c, y = lax.axis_index("rows"), lax.axis_index("cols"), lax.axis_index("depth")
    z_hi, x = r // NX, r % NX
    z_lo, core = c // 2, c % 2
    half = tok.shape[-1]
    f = held.shape[2]
    piece = half // 4
    weights = (w_gate_ref, w_up_ref, w_down_ref)
    sums, parts, parts_in = (sum_a, sum_b), (part_a, part_b), (in_a, in_b)
    acts, acts_other = (act_a, act_b), (other_a, other_b)

    def at(dz=0, dx=0, lo=None, k=None, dy=0):
        lo = z_lo if lo is None else lo
        k = core if k is None else k
        row = lax.rem(z_hi + dz, NQ) * NX + lax.rem(x + dx, NX)
        return (row, lo * 2 + k, lax.rem(y + dy, NY))

    def features(h):
        return pl.ds(pl.multiple_of((core + h) % 2 * half, half), half)

    for a, ref in enumerate((tokens_ref, cot_ref)):
        pltpu.make_async_copy(ref.at[:, features(0)], tok.at[0, a, 0, pl.ds(0, ROWS)], load_sem.at[2]).start()

    barrier = pltpu.get_barrier_semaphore()
    neighbour = at(k=1 - core)
    group = [(1 - z_lo, core), (z_lo, 1 - core), (1 - z_lo, 1 - core)]
    partners = [at(dx=d) for d in range(1, NX)] + [at(dy=d) for d in range(1, NY)]
    partners += [at(dz=d, lo=lo, k=k) for d in range(1, NQ) for lo in range(2) for k in range(2)]
    partners += [at(lo=lo, k=k) for lo, k in group]
    for partner in partners:
        pl.semaphore_signal(barrier, inc=1, device_id=partner, device_id_type=MESH)

    for h in range(2):
        for i, ref in enumerate(weights):
            pltpu.make_async_copy(ref.at[:, features(h)], held.at[h, i], load_sem.at[h]).start()

    own_shard = tok.at[0, :, 0, pl.ds(0, ROWS)]
    pltpu.make_async_copy(own_shard, own_shard, load_sem.at[2]).wait()
    pl.semaphore_wait(barrier, len(partners))

    Z, X, CORE, WEIGHT, SUM_A, SUM_B, ACT_A, ACT_B, PASS_A, PASS_B, OUT, NEAR, FAR = range(13)

    def send(src, dst, kind, rs, to):
        pltpu.make_async_remote_copy(
            src_ref=src, dst_ref=dst, send_sem=sent.at[kind], recv_sem=rs, device_id=to, device_id_type=MESH
        ).start()

    def arrived(dst, rs):
        pltpu.make_async_remote_copy(
            src_ref=dst, dst_ref=dst, send_sem=sent.at[0], recv_sem=rs, device_id=neighbour, device_id_type=MESH
        ).wait_recv()

    def left(size, kind):
        pltpu.make_async_remote_copy(
            src_ref=size, dst_ref=size, send_sem=sent.at[kind], recv_sem=wr.at[0], device_id=neighbour, device_id_type=MESH
        ).wait_send()

    def shard(a, q, p):
        return tok.at[0, a, q, pl.ds(p * ROWS, ROWS)]

    up = 3 - 2 * z_lo
    steps = (0, up, 2, NQ - up)

    def stage_z_in(a):
        send(shard(a, 0, 0), shard(a, 1, 0), Z, zr.at[a, 1], at(dz=up, lo=1 - z_lo))
        send(shard(a, 0, 0), shard(a, 3, 0), Z, zr.at[a, 3], at(dz=up))
        send(shard(a, 0, 0), shard(a, 2, 0), Z, zr.at[a, 2], at(dz=2, lo=1 - z_lo))

    def stage_x(a, q):
        if q:
            arrived(shard(a, q, 0), zr.at[a, q])
        for d in (2, 1, 3):
            send(shard(a, q, 0), shard(a, q, NX - d), X, xr.at[a, q], at(dx=d))

    def stage_core(a, q):
        arrived(tok.at[0, a, q, pl.ds(ROWS, 3 * ROWS)], xr.at[a, q])
        send(tok.at[0, a, q], tok.at[1, a, q], CORE, cr.at[a, q], neighbour)

    def stage_weights():
        for i in (2, 0, 1):
            send(weights[i].at[:, features(1)], other.at[i], WEIGHT, wr.at[0], neighbour)

    rows = NX * ROWS
    share = rows // NY

    def stage_mm(a, n, h, first):
        if first:
            pltpu.make_async_copy(held.at[h], held.at[h], load_sem.at[h]).wait()
        if h:
            arrived(tok.at[1, a, n], cr.at[a, n])
        w = held[h, 2] if a else held[h, 0:2].reshape(2 * f, half)
        term = contract_last(tok[h, a, n], w).reshape(NY, share, -1)
        if h:
            term = term + sums[a][n]
            parts[a][n] = term.astype(BF16)
        sums[a][n] = term
        if h:
            for d in (2, 1, 3):
                to = lax.rem(y + d, NY)
                send(parts[a].at[n, to], parts_in[a].at[n, NY - d - 1], SUM_A + a, yr.at[a, n], at(dy=d))

    def stage_act(a, n):
        arrived(parts_in[a].at[n], yr.at[a, n])
        into = parts_in[a]
        total = sums[a][n, y] + (into[n, 0].astype(F32) + into[n, 1].astype(F32) + into[n, 2].astype(F32))
        if a == 0:
            sum_a[n, y] = total
            gate, up_sum = total[:, :f], total[:, f:]
            act_a[n, y] = (gate * jax.nn.sigmoid(gate) * up_sum).astype(BF16)
        else:
            gate, up_sum = sum_a[n, y, :, :f], sum_a[n, y, :, f:]
            sigma = jax.nn.sigmoid(gate)
            gate_back = total * up_sum * sigma * (1.0 + gate * (1.0 - sigma))
            act_b[n, y] = jnp.concatenate([gate_back, total * gate * sigma], axis=1).astype(BF16)
        for d in (2, 1, 3):
            send(acts[a].at[n, y], acts[a].at[n, y], ACT_A + a, hr.at[a, n], at(dy=d))

    def stage_pass(a, n):
        arrived(parts_in[1 - a].at[n], hr.at[a, n])
        send(acts[a].at[n], acts_other[a].at[n], PASS_A + a, kr.at[a, n], neighbour)

    def stage_out(a, n, first):
        def output(ref, w):
            left_side = ref[n].reshape(rows, -1)
            return matmul(left_side, w[0:2].reshape(2 * f, half) if a else w[2])

        if first:
            arrived(other, wr.at[0])
        arrived(acts_other[a].at[n], kr.at[a, n])
        value = (output(acts[a], held.at[0]) + output(acts_other[a], other)).reshape(NX, ROWS, half)
        own[n, a] = value[0]
        xsend[n, a] = value[1:].astype(BF16)
        for d in (2, 1, 3):
            send(xsend.at[n, a, d - 1], xin.at[n, a, NX - d - 1], OUT, ur.at[a, n], at(dx=d))

    step = ROWS // 4

    def stage_z(a, n):
        arrived(xin.at[n, a], ur.at[a, n])
        value = own[n, a] + (xin[n, a, 0].astype(F32) + xin[n, a, 1].astype(F32) + xin[n, a, 2].astype(F32))
        for k in range(4):
            for j in range(4):
                zf[n, a, k, j * step:(j + 1) * step] = value[k * step:(k + 1) * step, j * piece:(j + 1) * piece]
        zsend[n, a] = zf[n, a].astype(BF16)
        if n == 0:
            for m, (lo, k) in enumerate(group):
                send(zsend.at[0, a, lo * 2 + k], zin.at[0, a, m + 1], NEAR, vr.at[a, 0], at(lo=lo, k=k))
        else:
            for differs in (1, 0) if n == 3 else (0, 1):
                lo = 1 - z_lo if differs else z_lo
                back = 2 if n == 2 else 1 if differs == (n == 1) else 3
                for k in range(2):
                    send(zsend.at[n, a, lo * 2 + k], zin.at[back, a, c], FAR, vr.at[a, back], at(dz=steps[n], lo=lo, k=k))

    def last(a, ref):
        arrived(zin.at[0, a, pl.ds(1, 3)], vr.at[a, 0])
        same = zf[0, a, c] + zin[0, a, 1].astype(F32)
        cross = zin[0, a, 2].astype(F32) + zin[0, a, 3].astype(F32)
        totals = [jnp.where(core == 0, same, cross), jnp.where(core == 0, cross, same)]
        for q in ORDER[1:]:
            arrived(zin.at[q, a], vr.at[a, q])
            for k in range(2):
                totals[k] = totals[k] + (zin[q, a, k].astype(F32) + zin[q, a, 2 + k].astype(F32))
        for k in range(2):
            for j in range(4):
                ref[:, k * half + j * piece:k * half + (j + 1) * piece] = (
                    totals[k][j * step:(j + 1) * step].astype(BF16)
                )

    def stage_grad(i, h):
        held_act = act_a[...] if i == 2 else act_b[:, :, :, i * f:(i + 1) * f]
        left_side = held_act.reshape(NQ * rows, f)
        for j in range(2):
            right_side = tok[h, i // 2, :, :, j * half // 2:(j + 1) * half // 2].reshape(NQ * rows, half // 2)
            place = pl.multiple_of((core + h) % 2 * half + j * half // 2, half // 2)
            (gate_grad, up_grad, down_grad)[i][:, pl.ds(place, half // 2)] = contract_first(left_side, right_side).astype(BF16)

    stage_z_in(0)
    stage_x(0, 0)
    stage_weights()
    stage_x(1, 0)
    stage_z_in(1)
    stage_x(0, 1)
    stage_x(0, 3)
    stage_core(0, 0)
    stage_core(1, 0)
    stage_x(0, 2)
    stage_mm(0, 0, 0, True)
    stage_mm(0, 0, 1, True)
    stage_x(1, 3)
    stage_core(0, 1)
    stage_mm(1, 0, 0, False)
    stage_mm(0, 1, 0, False)
    stage_mm(1, 0, 1, False)
    stage_x(1, 2)
    stage_core(0, 3)
    stage_mm(0, 1, 1, False)
    stage_x(1, 1)
    stage_mm(0, 3, 0, False)
    stage_core(0, 2)
    stage_mm(0, 3, 1, False)
    stage_mm(0, 2, 0, False)
    stage_core(1, 3)
    stage_mm(0, 2, 1, False)
    stage_mm(1, 3, 0, False)
    stage_core(1, 2)
    stage_act(0, 0)
    stage_mm(1, 2, 0, False)
    stage_act(0, 1)
    stage_mm(1, 2, 1, False)
    stage_core(1, 1)
    stage_mm(1, 1, 0, False)
    stage_mm(1, 3, 1, False)
    stage_act(0, 3)
    stage_act(0, 2)
    stage_mm(1, 1, 1, False)
    stage_pass(0, 0)
    stage_pass(0, 1)
    stage_act(1, 2)
    stage_out(0, 0, True)
    stage_act(1, 3)
    stage_out(0, 1, False)
    stage_pass(0, 2)
    stage_pass(0, 3)
    stage_act(1, 1)
    stage_act(1, 0)
    stage_out(0, 2, False)
    stage_pass(1, 2)
    stage_out(0, 3, False)
    stage_pass(1, 3)
    stage_z(0, 0)
    stage_out(1, 2, False)
    stage_pass(1, 1)
    stage_out(1, 3, False)
    stage_pass(1, 0)
    stage_out(1, 1, False)
    stage_z(0, 2)
    stage_out(1, 0, False)
    stage_z(0, 1)
    stage_z(0, 3)
    stage_grad(2, 0)
    stage_grad(2, 1)
    stage_z(1, 2)
    stage_grad(0, 0)
    stage_z(1, 3)
    stage_z(1, 1)
    stage_z(1, 0)
    stage_grad(0, 1)
    stage_grad(1, 0)
    stage_grad(1, 1)
    last(0, out_ref)
    last(1, back_ref)
    left(tok.at[0, :, 0, pl.ds(0, 3 * ROWS)], Z)
    left(tok.at[0, :, pl.ds(0, 3)], X)
    left(tok.at[0], CORE)
    left(other, WEIGHT)
    left(in_a, SUM_A)
    left(in_b, SUM_B)
    left(in_b, ACT_A)
    left(in_a, ACT_B)
    left(act_a, PASS_A)
    left(act_b, PASS_B)
    left(xin, OUT)
    left(zin.at[0, :, pl.ds(1, 3)], NEAR)
    left(zin.at[pl.ds(1, 3)], FAR)


def write_kernel(*refs):
    n = len(refs) // 2
    copies = [pltpu.make_async_copy(refs[i], refs[n + i], refs[-1].at[i]) for i in range(n)]
    for copy in copies:
        copy.start()
    for copy in copies:
        copy.wait()


def write_out(arrays):
    n = len(arrays)
    return pl.pallas_call(
        write_kernel,
        out_shape=[jax.ShapeDtypeStruct(v.shape, v.dtype) for v in arrays],
        in_specs=[pl.BlockSpec(memory_space=pl.ANY)] * n,
        out_specs=[pl.BlockSpec(memory_space=pl.ANY)] * n,
        scratch_shapes=[pltpu.SemaphoreType.DMA((n,))],
        compiler_params=pltpu.CompilerParams(vmem_limit_bytes=2**20),
        name="write",
    )(*arrays)


def on_device(tokens_in, cotangent, w_gate, w_up, w_down):
    d, f = w_gate.shape
    half = d // 2
    piece = half // 4
    group = NX * ROWS
    share = group // NY
    tokens = NQ * group
    dma = pltpu.SemaphoreType.DMA
    vmem = pl.BlockSpec(memory_space=pltpu.VMEM)
    hbm = pl.BlockSpec(memory_space=pltpu.HBM)
    results = pl.pallas_call(
        block_kernel,
        out_shape=[
            jax.ShapeDtypeStruct((4, d), BF16),
            jax.ShapeDtypeStruct((4, d), BF16),
            jax.ShapeDtypeStruct((f, d), BF16),
            jax.ShapeDtypeStruct((f, d), BF16),
            jax.ShapeDtypeStruct((f, d), BF16),
        ],
        in_specs=[hbm] * 5,
        out_specs=[vmem] * 5,
        scratch_shapes=[
            pltpu.VMEM((2, 2, NQ, group, half), BF16),
            pltpu.VMEM((2, 3, f, half), BF16),
            pltpu.VMEM((3, f, half), BF16),
            pltpu.VMEM((NQ, NY, share, 2 * f), F32),
            pltpu.VMEM((NQ, NY, share, f), F32),
            pltpu.VMEM((NQ, NY, share, 2 * f), BF16),
            pltpu.VMEM((NQ, NY, share, f), BF16),
            pltpu.VMEM((NQ, NY - 1, share, 2 * f), BF16),
            pltpu.VMEM((NQ, NY - 1, share, f), BF16),
            pltpu.VMEM((NQ, NY, share, f), BF16),
            pltpu.VMEM((NQ, NY, share, 2 * f), BF16),
            pltpu.VMEM((NQ, NY, share, f), BF16),
            pltpu.VMEM((NQ, NY, share, 2 * f), BF16),
            pltpu.VMEM((NQ, 2, ROWS, half), F32),
            pltpu.VMEM((NQ, 2, NX - 1, ROWS, half), BF16),
            pltpu.VMEM((NQ, 2, NX - 1, ROWS, half), BF16),
            pltpu.VMEM((NQ, 2, 4, ROWS, piece), F32),
            pltpu.VMEM((NQ, 2, 4, ROWS, piece), BF16),
            pltpu.VMEM((NQ, 2, 4, ROWS, piece), BF16),
            dma((3,)),
            dma((13,)),
            dma((1,)),
            dma((2, NQ)),
            dma((2, NQ)),
            dma((2, NQ)),
            dma((2, NQ)),
            dma((2, NQ)),
            dma((2, NQ)),
            dma((2, NQ)),
            dma((2, NQ)),
        ],
        compiler_params=pltpu.CompilerParams(
            collective_id=0, has_side_effects=True, vmem_limit_bytes=40 * 2**20
        ),
        cost_estimate=pl.CostEstimate(flops=12 * tokens * d * f, bytes_accessed=6 * d * f, transcendentals=tokens * f),
        name="block",
    )(*[
        pltpu.with_memory_space_constraint(v, pltpu.HBM)
        for v in (tokens_in, cotangent, w_gate.T, w_up.T, w_down)
    ])
    out, back, gate_grad, up_grad, down_grad = write_out(results)
    return (out, back, gate_grad.T, up_grad.T, down_grad)


def solution(mesh):
    return jax.shard_map(
        on_device,
        mesh=mesh,
        in_specs=(
            P("rows", "depth"),
            P("rows", "depth"),
            P("depth", ("rows", "cols")),
            P("depth", ("rows", "cols")),
            P(("rows", "cols"), "depth"),
        ),
        out_specs=(
            P(("rows", "cols"), "depth"),
            P(("rows", "cols"), "depth"),
            P("depth", ("rows", "cols")),
            P("depth", ("rows", "cols")),
            P(("rows", "cols"), "depth"),
        ),
        check_vma=False,
    )
```

```python
import functools

import jax
import jax.numpy as jnp
from jax import lax
from jax.experimental import pallas as pl
from jax.experimental.pallas import tpu as pltpu
from jax.sharding import PartitionSpec as P

MESH = pl.DeviceIdType.MESH
F32 = jnp.float32
BF16 = jnp.bfloat16
NQ = 4
NX = 4
NY = 4
ORDER = [0, 1, 3, 2]
ROWS = 16


def contract_last(left, right):
    return lax.dot_general(
        left, right, (((1,), (1,)), ((), ())), preferred_element_type=F32
    )


def matmul(left, right):
    return jnp.dot(left, right, preferred_element_type=F32)


def contract_first(left, right):
    return lax.dot_general(
        left, right, (((0,), (0,)), ((), ())), preferred_element_type=F32
    )


def block_kernel(
    tokens_ref, cot_ref, w_gate_ref, w_up_ref, w_down_ref,
    out_ref, back_ref, gate_grad, up_grad, down_grad,
    tok, held, other, sum_a, sum_b, part_a, part_b, in_a, in_b, act_a, act_b, other_a, other_b,
    own, xsend, xin, zf, zsend, zin,
    load_sem, sent, wr, zr, xr, cr, yr, hr, kr, ur, vr,
):
    r, c, y = lax.axis_index("rows"), lax.axis_index("cols"), lax.axis_index("depth")
    z_hi, x = r // NX, r % NX
    z_lo, core = c // 2, c % 2
    half = tok.shape[-1]
    f = held.shape[2]
    piece = half // 4
    weights = (w_gate_ref, w_up_ref, w_down_ref)
    sums, parts, parts_in = (sum_a, sum_b), (part_a, part_b), (in_a, in_b)
    acts, acts_other = (act_a, act_b), (other_a, other_b)

    def at(dz=0, dx=0, lo=None, k=None, dy=0):
        lo = z_lo if lo is None else lo
        k = core if k is None else k
        row = lax.rem(z_hi + dz, NQ) * NX + lax.rem(x + dx, NX)
        return (row, lo * 2 + k, lax.rem(y + dy, NY))

    def features(h):
        return pl.ds(pl.multiple_of((core + h) % 2 * half, half), half)

    for a, ref in enumerate((tokens_ref, cot_ref)):
        pltpu.make_async_copy(ref.at[:, features(0)], tok.at[0, a, 0, pl.ds(0, ROWS)], load_sem.at[2]).start()

    barrier = pltpu.get_barrier_semaphore()
    neighbour = at(k=1 - core)
    group = [(1 - z_lo, core), (z_lo, 1 - core), (1 - z_lo, 1 - core)]
    partners = [at(dx=d) for d in range(1, NX)] + [at(dy=d) for d in range(1, NY)]
    partners += [at(dz=d, lo=lo, k=k) for d in range(1, NQ) for lo in range(2) for k in range(2)]
    partners += [at(lo=lo, k=k) for lo, k in group]
    for partner in partners:
        pl.semaphore_signal(barrier, inc=1, device_id=partner, device_id_type=MESH)

    for h in range(2):
        for i, ref in enumerate(weights):
            pltpu.make_async_copy(ref.at[:, features(h)], held.at[h, i], load_sem.at[h]).start()

    own_shard = tok.at[0, :, 0, pl.ds(0, ROWS)]
    pltpu.make_async_copy(own_shard, own_shard, load_sem.at[2]).wait()
    pl.semaphore_wait(barrier, len(partners))

    Z, X, CORE, WEIGHT, SUM_A, SUM_B, ACT_A, ACT_B, PASS_A, PASS_B, OUT, NEAR, FAR = range(13)

    def send(src, dst, kind, rs, to):
        pltpu.make_async_remote_copy(
            src_ref=src, dst_ref=dst, send_sem=sent.at[kind], recv_sem=rs, device_id=to, device_id_type=MESH
        ).start()

    def arrived(dst, rs):
        pltpu.make_async_remote_copy(
            src_ref=dst, dst_ref=dst, send_sem=sent.at[0], recv_sem=rs, device_id=neighbour, device_id_type=MESH
        ).wait_recv()

    def left(size, kind):
        pltpu.make_async_remote_copy(
            src_ref=size, dst_ref=size, send_sem=sent.at[kind], recv_sem=wr.at[0], device_id=neighbour, device_id_type=MESH
        ).wait_send()

    def shard(a, q, p):
        return tok.at[0, a, q, pl.ds(p * ROWS, ROWS)]

    up = 3 - 2 * z_lo
    steps = (0, up, 2, NQ - up)

    def stage_z_in(a):
        hops = [(1, at(dz=up, lo=1 - z_lo)), (3, at(dz=up)), (2, at(dz=2, lo=1 - z_lo))]
        for q, to in hops[::-1] if a else hops:
            send(shard(a, 0, 0), shard(a, q, 0), Z, zr.at[a, q], to)

    def stage_x(a, q):
        if q:
            arrived(shard(a, q, 0), zr.at[a, q])
        for d in (2, 1, 3):
            send(shard(a, q, 0), shard(a, q, NX - d), X, xr.at[a, q], at(dx=d))

    def stage_core(a, q):
        arrived(tok.at[0, a, q, pl.ds(ROWS, 3 * ROWS)], xr.at[a, q])
        send(tok.at[0, a, q], tok.at[1, a, q], CORE, cr.at[a, q], neighbour)

    def stage_weights():
        for i in (2, 0, 1):
            send(weights[i].at[:, features(1)], other.at[i], WEIGHT, wr.at[0], neighbour)

    rows = NX * ROWS
    share = rows // NY

    def stage_mm(a, n, h, first):
        if first:
            pltpu.make_async_copy(held.at[h], held.at[h], load_sem.at[h]).wait()
        if h:
            arrived(tok.at[1, a, n], cr.at[a, n])
        w = held[h, 2] if a else held[h, 0:2].reshape(2 * f, half)
        term = contract_last(tok[h, a, n], w).reshape(NY, share, -1)
        if h:
            term = term + sums[a][n]
            parts[a][n] = term.astype(BF16)
        sums[a][n] = term
        if h:
            for d in (2, 1, 3):
                to = lax.rem(y + d, NY)
                send(parts[a].at[n, to], parts_in[a].at[n, NY - d - 1], SUM_A + a, yr.at[a, n], at(dy=d))

    def stage_act(a, n):
        arrived(parts_in[a].at[n], yr.at[a, n])
        into = parts_in[a]
        total = sums[a][n, y] + (into[n, 0].astype(F32) + into[n, 1].astype(F32) + into[n, 2].astype(F32))
        if a == 0:
            sum_a[n, y] = total
            gate, up_sum = total[:, :f], total[:, f:]
            act_a[n, y] = (gate * jax.nn.sigmoid(gate) * up_sum).astype(BF16)
        else:
            gate, up_sum = sum_a[n, y, :, :f], sum_a[n, y, :, f:]
            sigma = jax.nn.sigmoid(gate)
            gate_back = total * up_sum * sigma * (1.0 + gate * (1.0 - sigma))
            act_b[n, y] = jnp.concatenate([gate_back, total * gate * sigma], axis=1).astype(BF16)
        for d in (2, 1, 3):
            send(acts[a].at[n, y], acts[a].at[n, y], ACT_A + a, hr.at[a, n], at(dy=d))

    def stage_pass(a, n):
        arrived(parts_in[1 - a].at[n], hr.at[a, n])
        send(acts[a].at[n], acts_other[a].at[n], PASS_A + a, kr.at[a, n], neighbour)

    def stage_out(a, n, first):
        def output(ref, w):
            left_side = ref[n].reshape(rows, -1)
            return matmul(left_side, w[0:2].reshape(2 * f, half) if a else w[2])

        if first:
            arrived(other, wr.at[0])
        arrived(acts_other[a].at[n], kr.at[a, n])
        value = (output(acts[a], held.at[0]) + output(acts_other[a], other)).reshape(NX, ROWS, half)
        own[n, a] = value[0]
        xsend[n, a] = value[1:].astype(BF16)
        for d in (2, 1, 3):
            send(xsend.at[n, a, d - 1], xin.at[n, a, NX - d - 1], OUT, ur.at[a, n], at(dx=d))

    step = ROWS // 4

    def stage_z(a, n):
        arrived(xin.at[n, a], ur.at[a, n])
        value = own[n, a] + (xin[n, a, 0].astype(F32) + xin[n, a, 1].astype(F32) + xin[n, a, 2].astype(F32))
        for k in range(4):
            for j in range(4):
                zf[n, a, k, j * step:(j + 1) * step] = value[k * step:(k + 1) * step, j * piece:(j + 1) * piece]
        zsend[n, a] = zf[n, a].astype(BF16)
        if n == 0:
            for m, (lo, k) in enumerate(group):
                send(zsend.at[0, a, lo * 2 + k], zin.at[0, a, m + 1], NEAR, vr.at[a, 0], at(lo=lo, k=k))
        else:
            for differs in (1, 0) if n == 3 else (0, 1):
                lo = 1 - z_lo if differs else z_lo
                back = 2 if n == 2 else 1 if differs == (n == 1) else 3
                for k in range(2):
                    send(zsend.at[n, a, lo * 2 + k], zin.at[back, a, c], FAR, vr.at[a, back], at(dz=steps[n], lo=lo, k=k))

    def last(a, ref):
        arrived(zin.at[0, a, pl.ds(1, 3)], vr.at[a, 0])
        same = zf[0, a, c] + zin[0, a, 1].astype(F32)
        cross = zin[0, a, 2].astype(F32) + zin[0, a, 3].astype(F32)
        totals = [jnp.where(core == 0, same, cross), jnp.where(core == 0, cross, same)]
        for q in ORDER[1:]:
            arrived(zin.at[q, a], vr.at[a, q])
            for k in range(2):
                totals[k] = totals[k] + (zin[q, a, k].astype(F32) + zin[q, a, 2 + k].astype(F32))
        for k in range(2):
            for j in range(4):
                ref[:, k * half + j * piece:k * half + (j + 1) * piece] = (
                    totals[k][j * step:(j + 1) * step].astype(BF16)
                )

    def stage_grad(i, h):
        held_act = act_a[...] if i == 2 else act_b[:, :, :, i * f:(i + 1) * f]
        left_side = held_act.reshape(NQ * rows, f)
        for j in range(2):
            right_side = tok[h, i // 2, :, :, j * half // 2:(j + 1) * half // 2].reshape(NQ * rows, half // 2)
            place = pl.multiple_of((core + h) % 2 * half + j * half // 2, half // 2)
            (gate_grad, up_grad, down_grad)[i][:, pl.ds(place, half // 2)] = contract_first(left_side, right_side).astype(BF16)

    stage_z_in(0)
    stage_x(0, 0)
    stage_weights()
    stage_x(1, 0)
    stage_z_in(1)
    stage_x(0, 1)
    stage_x(0, 3)
    stage_core(0, 0)
    stage_core(1, 0)
    stage_x(0, 2)
    stage_mm(0, 0, 0, True)
    stage_mm(0, 0, 1, True)
    stage_x(1, 3)
    stage_core(0, 1)
    stage_mm(1, 0, 0, False)
    stage_mm(0, 1, 0, False)
    stage_mm(1, 0, 1, False)
    stage_x(1, 2)
    stage_core(0, 3)
    stage_mm(0, 1, 1, False)
    stage_x(1, 1)
    stage_mm(0, 3, 0, False)
    stage_core(0, 2)
    stage_mm(0, 3, 1, False)
    stage_mm(0, 2, 0, False)
    stage_core(1, 3)
    stage_mm(0, 2, 1, False)
    stage_mm(1, 3, 0, False)
    stage_core(1, 2)
    stage_act(0, 0)
    stage_mm(1, 2, 0, False)
    stage_act(0, 1)
    stage_mm(1, 2, 1, False)
    stage_core(1, 1)
    stage_mm(1, 1, 0, False)
    stage_mm(1, 3, 1, False)
    stage_act(0, 3)
    stage_act(0, 2)
    stage_mm(1, 1, 1, False)
    stage_pass(0, 0)
    stage_pass(0, 1)
    stage_act(1, 2)
    stage_out(0, 0, True)
    stage_act(1, 3)
    stage_out(0, 1, False)
    stage_pass(0, 2)
    stage_pass(0, 3)
    stage_act(1, 1)
    stage_act(1, 0)
    stage_out(0, 2, False)
    stage_pass(1, 2)
    stage_out(0, 3, False)
    stage_pass(1, 3)
    stage_z(0, 0)
    stage_out(1, 2, False)
    stage_pass(1, 1)
    stage_out(1, 3, False)
    stage_pass(1, 0)
    stage_out(1, 1, False)
    stage_z(0, 2)
    stage_out(1, 0, False)
    stage_z(0, 1)
    stage_z(0, 3)
    stage_grad(2, 0)
    stage_grad(2, 1)
    stage_z(1, 2)
    stage_grad(0, 0)
    stage_z(1, 3)
    stage_z(1, 1)
    stage_z(1, 0)
    stage_grad(0, 1)
    stage_grad(1, 0)
    stage_grad(1, 1)
    last(0, out_ref)
    last(1, back_ref)
    left(tok.at[0, :, 0, pl.ds(0, 3 * ROWS)], Z)
    left(tok.at[0, :, pl.ds(0, 3)], X)
    left(tok.at[0], CORE)
    left(other, WEIGHT)
    left(in_a, SUM_A)
    left(in_b, SUM_B)
    left(in_b, ACT_A)
    left(in_a, ACT_B)
    left(act_a, PASS_A)
    left(act_b, PASS_B)
    left(xin, OUT)
    left(zin.at[0, :, pl.ds(1, 3)], NEAR)
    left(zin.at[pl.ds(1, 3)], FAR)


def write_kernel(*refs):
    n = len(refs) // 2
    copies = [pltpu.make_async_copy(refs[i], refs[n + i], refs[-1].at[i]) for i in range(n)]
    for copy in copies:
        copy.start()
    for copy in copies:
        copy.wait()


def write_out(arrays):
    n = len(arrays)
    return pl.pallas_call(
        write_kernel,
        out_shape=[jax.ShapeDtypeStruct(v.shape, v.dtype) for v in arrays],
        in_specs=[pl.BlockSpec(memory_space=pl.ANY)] * n,
        out_specs=[pl.BlockSpec(memory_space=pl.ANY)] * n,
        scratch_shapes=[pltpu.SemaphoreType.DMA((n,))],
        compiler_params=pltpu.CompilerParams(vmem_limit_bytes=2**20),
        name="write",
    )(*arrays)


def on_device(tokens_in, cotangent, w_gate, w_up, w_down):
    d, f = w_gate.shape
    half = d // 2
    piece = half // 4
    group = NX * ROWS
    share = group // NY
    tokens = NQ * group
    dma = pltpu.SemaphoreType.DMA
    vmem = pl.BlockSpec(memory_space=pltpu.VMEM)
    hbm = pl.BlockSpec(memory_space=pltpu.HBM)
    results = pl.pallas_call(
        block_kernel,
        out_shape=[
            jax.ShapeDtypeStruct((4, d), BF16),
            jax.ShapeDtypeStruct((4, d), BF16),
            jax.ShapeDtypeStruct((f, d), BF16),
            jax.ShapeDtypeStruct((f, d), BF16),
            jax.ShapeDtypeStruct((f, d), BF16),
        ],
        in_specs=[hbm] * 5,
        out_specs=[vmem] * 5,
        scratch_shapes=[
            pltpu.VMEM((2, 2, NQ, group, half), BF16),
            pltpu.VMEM((2, 3, f, half), BF16),
            pltpu.VMEM((3, f, half), BF16),
            pltpu.VMEM((NQ, NY, share, 2 * f), F32),
            pltpu.VMEM((NQ, NY, share, f), F32),
            pltpu.VMEM((NQ, NY, share, 2 * f), BF16),
            pltpu.VMEM((NQ, NY, share, f), BF16),
            pltpu.VMEM((NQ, NY - 1, share, 2 * f), BF16),
            pltpu.VMEM((NQ, NY - 1, share, f), BF16),
            pltpu.VMEM((NQ, NY, share, f), BF16),
            pltpu.VMEM((NQ, NY, share, 2 * f), BF16),
            pltpu.VMEM((NQ, NY, share, f), BF16),
            pltpu.VMEM((NQ, NY, share, 2 * f), BF16),
            pltpu.VMEM((NQ, 2, ROWS, half), F32),
            pltpu.VMEM((NQ, 2, NX - 1, ROWS, half), BF16),
            pltpu.VMEM((NQ, 2, NX - 1, ROWS, half), BF16),
            pltpu.VMEM((NQ, 2, 4, ROWS, piece), F32),
            pltpu.VMEM((NQ, 2, 4, ROWS, piece), BF16),
            pltpu.VMEM((NQ, 2, 4, ROWS, piece), BF16),
            dma((3,)),
            dma((13,)),
            dma((1,)),
            dma((2, NQ)),
            dma((2, NQ)),
            dma((2, NQ)),
            dma((2, NQ)),
            dma((2, NQ)),
            dma((2, NQ)),
            dma((2, NQ)),
            dma((2, NQ)),
        ],
        compiler_params=pltpu.CompilerParams(
            collective_id=0, has_side_effects=True, vmem_limit_bytes=40 * 2**20
        ),
        cost_estimate=pl.CostEstimate(flops=12 * tokens * d * f, bytes_accessed=6 * d * f, transcendentals=tokens * f),
        name="block",
    )(*[
        pltpu.with_memory_space_constraint(v, pltpu.HBM)
        for v in (tokens_in, cotangent, w_gate.T, w_up.T, w_down)
    ])
    out, back, gate_grad, up_grad, down_grad = write_out(results)
    return (out, back, gate_grad.T, up_grad.T, down_grad)


def solution(mesh):
    return jax.shard_map(
        on_device,
        mesh=mesh,
        in_specs=(
            P("rows", "depth"),
            P("rows", "depth"),
            P("depth", ("rows", "cols")),
            P("depth", ("rows", "cols")),
            P(("rows", "cols"), "depth"),
        ),
        out_specs=(
            P(("rows", "cols"), "depth"),
            P(("rows", "cols"), "depth"),
            P("depth", ("rows", "cols")),
            P("depth", ("rows", "cols")),
            P(("rows", "cols"), "depth"),
        ),
        check_vma=False,
    )
```
